32 devices in a mesh: segment: 4 (over x, core), patch: 8 (over z, y).
Axes of the slice: x: 2, y: 2, z: 4, core: 2. Of those that a mesh axis runs over, the one named last changes fastest.
Arguments:
- features: bfloat16 [32, 28, 4, 12, 128], P('patch'), may hold values from -6 to 6
- deep_path: bfloat16 [32, 28, 4, 12, 128], P('patch'), may hold values from -6 to 6
- weight_first: bfloat16 [9, 28, 28], replicated, may hold values from -0.375 to 0.375
- bias_first: float32 [28], replicated, may hold values from -3 to 3
- weight_second: bfloat16 [27, 28, 28], replicated, may hold values from -0.21875 to 0.21875
- bias_second: float32 [28], replicated, may hold values from -3 to 3
- weight_third: bfloat16 [27, 28, 56], replicated, may hold values from -0.15625 to 0.15625
- bias_third: float32 [28], replicated, may hold values from -3 to 3
- weight_fourth: bfloat16 [27, 28, 56], replicated, may hold values from -0.15625 to 0.15625
- bias_fourth: float32 [28], replicated, may hold values from -3 to 3
- head_weight: bfloat16 [3, 28], replicated, may hold values from -2 to 2
- head_bias: float32 [3], replicated, may hold values from -3 to 3
- block_first: int32 [32], replicated, may hold values from 0 to 60, as said below
- block_offset: int32 [32], replicated, may hold values from 0 to 3
Outputs:
- blended: float32 [8, 8, 3, 4, 4, 128], P(None, 'patch', None, 'segment')
The draws below stay inside these ranges and needn't reach their ends.
Inputs may be any that keep to these rules, and one draw needn't show every extreme that they name: A patch touches only blocks block_first to block_first + 3, all inside the slab.
All inputs are finite; a program needn't handle non-finite values.
Results may differ from the reference program's by a relative error of at most 0.0022.
Values may be sent and summed in bfloat16 or wider, within the bound.
No kernel may reach another device: no remote copies, remote signals or barrier semaphores. Data moves between devices by JAX's collectives and lax.ppermute only.
A program may use at most 64 MiB of HBM per device.

```python
import jax
import jax.numpy as jnp
from jax import lax

C = 28
CD = 56
PZ = 4
PA = 12
PY = 128
CW = 4
CH_DEV = 8
KMAX = 4
PATCHES = 32
OWNERS = 8
NCHUNK = 64


def draw_block_first(key, part):
    top = NCHUNK - KMAX
    key_left, key_right, key_pick = jax.random.split(key, 3)
    left = jax.random.randint(key_left, (PATCHES,), 0, top + 1)
    right = jax.random.randint(key_right, (PATCHES,), 0, top + 1)
    first = jnp.minimum(left, right)
    picks = jax.random.permutation(key_pick, PATCHES)
    index = jnp.arange(PATCHES)
    first = jnp.where(index == picks[0], top, first)
    first = jnp.where(index == picks[1], 0, first)
    return first.astype(jnp.int32)


def place_ends(drawn, rng, low, high):
    spot = [jax.random.randint(jax.random.fold_in(rng, axis), (), 0, length) for axis, length in enumerate(drawn.shape)]
    longest = drawn.shape.index(max(drawn.shape))
    neighbour = spot[:longest] + [(spot[longest] + 1) % drawn.shape[longest]] + spot[longest + 1:]
    return drawn.at[tuple(spot)].set(low).at[tuple(neighbour)].set(high)


def block_levels(stream_key, shape, cuts, low, top_value):
    def one(dim, blocks):
        steps = jax.random.uniform(jax.random.fold_in(jax.random.fold_in(stream_key, 6), dim), (blocks,), jnp.float32, low / len(cuts), top_value / len(cuts))
        return jnp.repeat(jnp.exp(steps), shape[dim] // blocks).reshape((-1,) + (1,) * (len(shape) - dim - 1))

    level = one(*cuts[0])
    for cut in cuts[1:]:
        level = level * one(*cut)
    return level


def bell_draw(rng, extent, scale, reach, cuts=(), kind=jnp.bfloat16):
    entries = jax.random.normal(rng, extent, jnp.float32) * scale
    if len(cuts) > 0:
        entries = block_levels(rng, extent, cuts, -0.22, 0.18) * entries
    return jnp.clip(entries, min=-reach, max=reach).astype(kind)


def setup_inputs(seed: int = 0) -> dict:
    keys = jax.random.split(jax.random.key(seed), 15)
    return {
        "features": bell_draw(keys[0], (PATCHES, C, PZ, PA, PY), 1.0, 6.0, ((0, 8),)),
        "deep_path": bell_draw(keys[1], (PATCHES, C, PZ, PA, PY), 1.0, 6.0, ((0, 8),)),
        "weight_first": bell_draw(keys[2], (9, C, C), (9 * C) ** -0.5, 0.375),
        "bias_first": bell_draw(keys[3], (C,), 0.5, 3.0, (), jnp.float32),
        "weight_second": bell_draw(keys[4], (27, C, C), (27 * C) ** -0.5, 0.21875),
        "bias_second": bell_draw(keys[5], (C,), 0.5, 3.0, (), jnp.float32),
        "weight_third": bell_draw(keys[6], (27, C, CD), (27 * CD) ** -0.5, 0.15625),
        "bias_third": bell_draw(keys[7], (C,), 0.5, 3.0, (), jnp.float32),
        "weight_fourth": bell_draw(keys[8], (27, C, CD), (27 * CD) ** -0.5, 0.15625),
        "bias_fourth": bell_draw(keys[9], (C,), 0.5, 3.0, (), jnp.float32),
        "head_weight": bell_draw(keys[10], (3, C), (C // 4) ** -0.5, 2.0),
        "head_bias": bell_draw(keys[11], (3,), 1.0, 3.0, (), jnp.float32),
        "block_first": draw_block_first(jax.random.fold_in(keys[14], 71), 0),
        "block_offset": place_ends(jax.random.randint(keys[13], (PATCHES,), 0, CW), jax.random.fold_in(keys[13], 1), 0, CW - 1).astype(jnp.int32),
    }


def bump(count):
    place = (jnp.arange(count).astype(jnp.float32) + 0.5) / count
    return jnp.sin(jnp.pi * place) ** 2


def blend_window(depth, along, across):
    return bump(depth)[:, None, None] * bump(along)[None, :, None] * bump(across)[None, None, :]


def convolve_plane(source, kernel):
    depth, along, across = source.shape[1], source.shape[2], source.shape[3]
    padded = jnp.pad(source, ((0, 0), (0, 0), (1, 1), (1, 1))).astype(jnp.float32)
    total = jnp.zeros((kernel.shape[1], depth, along, across), jnp.float32)
    for row_shift in range(3):
        for col_shift in range(3):
            window = padded[:, :, row_shift:row_shift + along, col_shift:col_shift + across]
            total = total + jnp.einsum("oc,czay->ozay", kernel[row_shift * 3 + col_shift].astype(jnp.float32), window)
    return total


def convolve_full(source, kernel):
    depth, along, across = source.shape[1], source.shape[2], source.shape[3]
    padded = jnp.pad(source, ((0, 0), (1, 1), (1, 1), (1, 1))).astype(jnp.float32)
    total = jnp.zeros((kernel.shape[1], depth, along, across), jnp.float32)
    for depth_shift in range(3):
        for row_shift in range(3):
            for col_shift in range(3):
                window = padded[:, depth_shift:depth_shift + depth, row_shift:row_shift + along, col_shift:col_shift + across]
                total = total + jnp.einsum("oc,czay->ozay", kernel[depth_shift * 9 + row_shift * 3 + col_shift].astype(jnp.float32), window)
    return total


def layer(total, bias):
    return jax.nn.relu(total + bias[:, None, None, None]).astype(jnp.bfloat16)


def reference(features, deep_path, weight_first, bias_first, weight_second, bias_second, weight_third, bias_third, weight_fourth, bias_fourth, head_weight, head_bias, block_first, block_offset):
    window = blend_window(PZ, PA, PY)

    def accumulate(slab, items):
        patch_in, deep_in, first_block, offset = items
        first = layer(convolve_plane(patch_in, weight_first), bias_first)
        second = layer(convolve_full(first, weight_second), bias_second)
        third = layer(convolve_full(jnp.concatenate([second, deep_in], axis=0), weight_third), bias_third)
        fourth = layer(convolve_full(jnp.concatenate([third, first], axis=0), weight_fourth), bias_fourth)
        logits = jnp.einsum("oc,czay->ozay", head_weight.astype(jnp.float32), fourth.astype(jnp.float32)) + head_bias[:, None, None, None]
        partial_value = jax.nn.sigmoid(logits) * window
        start = (first_block * CW + offset).astype(jnp.int32)
        zero = jnp.zeros((), jnp.int32)
        current = lax.dynamic_slice(slab, (zero, zero, start, zero), partial_value.shape)
        return lax.dynamic_update_slice(slab, current + partial_value, (zero, zero, start, zero)), None

    slab = jnp.zeros((3, PZ, NCHUNK * CW, PY), jnp.float32)
    slab, unused = lax.scan(accumulate, slab, (features, deep_path, block_first, block_offset))
    return slab.reshape(3, PZ, CH_DEV, OWNERS, CW, PY).transpose(2, 3, 0, 1, 4, 5)
```

```python
import functools
import math

import jax
import jax.numpy as jnp
import numpy as np
from jax import lax
from jax.experimental import pallas as pl
from jax.experimental.pallas import tpu as pltpu
from jax.sharding import PartitionSpec as P

CW = 4
CH_DEV = 8
KMAX = 4
LANES = 128
SLOT = 32
GROUP = 4
BF = jnp.bfloat16
F32 = jnp.float32


def bump(count):
    place = (np.arange(count).astype(np.float32) + np.float32(0.5)) / np.float32(count)
    return (np.sin(np.float32(np.pi) * place) ** 2).astype(np.float32)


def lane_index(rows):
    return lax.broadcasted_iota(jnp.int32, (rows, LANES), 1)


def put_shifted(act, row, value):
    rows = value.shape[0]
    lane = lane_index(rows)
    act[1, pl.ds(row, rows), :] = value.astype(BF)
    act[0, pl.ds(row, rows), :] = jnp.where(lane == 0, 0.0, pltpu.roll(value, 1, 1)).astype(BF)
    act[2, pl.ds(row, rows), :] = jnp.where(
        lane == LANES - 1, 0.0, pltpu.roll(value, LANES - 1, 1)
    ).astype(BF)


def build_taps(weight, low, chans, strip, big, depth):
    lane = lane_index(SLOT)
    for dy in range(3):
        for da in range(3):
            k = dy * 3 + da
            for dz in range(3):
                strip[k, 0:chans, dz * SLOT : dz * SLOT + chans] = weight[
                    9 * dz + 3 * da + dy, :, low : low + chans
                ].astype(F32)
            base = strip[k]
            for z in range(depth):
                shift = ((z - 1) * SLOT) % LANES
                moved = pltpu.roll(base, shift, 1) if shift else base
                if z == 0:
                    moved = jnp.where(lane < LANES - SLOT, moved, 0.0)
                if z == depth - 1:
                    moved = jnp.where(lane >= SLOT, moved, 0.0)
                big[z * SLOT : (z + 1) * SLOT, k * LANES : (k + 1) * LANES] = moved.astype(BF)


def column(row_ref, pad, rows, pick):
    pad[...] = jnp.zeros(pad.shape, F32)
    pad[0:1, 0 : row_ref.shape[1]] = row_ref[...]
    spread = jnp.broadcast_to(pad[0:1, :], (rows, LANES))
    want = pick(lax.broadcasted_iota(jnp.int32, (rows, LANES), 0))
    return jnp.sum(jnp.where(lane_index(rows) == want, spread, 0.0), axis=1, keepdims=True)


def unet_kernel(
    owners,
    first_block,
    offset,
    features,
    deep,
    w1,
    w2,
    w3,
    w4,
    b1,
    b2,
    b3,
    b4,
    hw,
    hb,
    wy,
    out,
    feat_v,
    deep_v,
    w1_v,
    w2_v,
    w3_v,
    w4_v,
    cells,
    xf,
    x1,
    x2,
    xd,
    x3,
    m1,
    m2,
    m3s,
    m3d,
    m4t,
    m4f,
    strip,
    pad,
    head,
    sems,
):
    chans, depth, along = feat_v.shape[0], feat_v.shape[1], feat_v.shape[2]
    plane = depth * SLOT
    me = lax.axis_index("segment")
    patch = lax.axis_index("patch") * features.shape[0] + me

    copies = [
        pltpu.make_async_copy(src, dst, sems.at[i])
        for i, (src, dst) in enumerate(
            [
                (features.at[me], feat_v),
                (w1, w1_v),
                (w2, w2_v),
                (deep.at[me], deep_v),
                (w3, w3_v),
                (w4, w4_v),
            ]
        )
    ]
    for c in copies:
        c.start()

    for act in (x1, x2, xd, x3):
        for dy in range(3):
            act[dy, 0:plane, :] = jnp.zeros((plane, LANES), BF)
            act[dy, (along + 1) * plane : (along + 2) * plane, :] = jnp.zeros((plane, LANES), BF)
    high = (along + 2) * SLOT
    for dy in range(3):
        for z in range(depth):
            xf[dy, z * high : z * high + SLOT, :] = jnp.zeros((SLOT, LANES), BF)
            xf[dy, (z + 1) * high - SLOT : (z + 1) * high, :] = jnp.zeros((SLOT, LANES), BF)
    m1[...] = jnp.zeros(m1.shape, F32)
    strip[...] = jnp.zeros(strip.shape, F32)
    head[...] = jnp.zeros(head.shape, F32)
    out[...] = jnp.zeros(out.shape, F32)
    rows16 = 16
    cells[chans * depth * rows16 :, :] = jnp.zeros(
        (cells.shape[0] - chans * depth * rows16, LANES), F32
    )

    def spread_cells(source):
        for c in range(chans):
            for z in range(depth):
                cells[pl.ds((c * depth + z) * rows16, along), :] = source[c, z].astype(F32)

    def gathered(z, a):
        return cells[pl.ds(z * rows16 + a, SLOT, stride=depth * rows16), :]

    def own(r):
        return r

    copies[0].wait()
    spread_cells(feat_v)
    for z in range(depth):
        for a in range(along):
            put_shifted(xf, z * high + (a + 1) * SLOT, gathered(z, a))

    copies[1].wait()
    span = (GROUP + 2) * SLOT
    for dy in range(3):
        for da in range(3):
            tap = w1_v[da * 3 + dy].astype(F32)
            for a in range(GROUP):
                lo = dy * span + (a + da) * SLOT
                m1[a * SLOT : a * SLOT + chans, lo : lo + chans] = tap
    m1_b = m1[...].astype(BF)

    def bias_rows(ref, copies_of):
        col = column(ref, pad, SLOT, own)
        tile = jnp.broadcast_to(col, (SLOT, LANES))
        return jnp.concatenate([tile] * copies_of, axis=0)

    bias = bias_rows(b1, GROUP)
    for z in range(depth):
        for pair in range(0, along // GROUP):
            rhs = jnp.concatenate(
                [xf[dy, pl.ds(z * high + pair * GROUP * SLOT, span), :] for dy in range(3)], axis=0
            )
            got = jnp.dot(m1_b, rhs, preferred_element_type=F32)
            got = jnp.maximum(got + bias, 0.0)
            for a in range(GROUP):
                put_shifted(
                    x1,
                    (1 + pair * GROUP + a) * plane + z * SLOT,
                    got[a * SLOT : (a + 1) * SLOT],
                )

    def window_of(act, a):
        return jnp.concatenate([act[dy, pl.ds(a * plane, 3 * plane), :] for dy in range(3)], axis=0)

    def conv(mats, acts, bias, a):
        matrix = jnp.concatenate([m[...] for m in mats], axis=1) if len(mats) > 1 else mats[0][...]
        cols = []
        for b in (a, a + 1):
            parts = [window_of(x, b) for x in acts]
            cols.append(jnp.concatenate(parts, axis=0) if len(parts) > 1 else parts[0])
        got = jnp.dot(matrix, jnp.concatenate(cols, axis=1), preferred_element_type=F32)
        wide = jnp.concatenate([bias, bias], axis=1)
        return jnp.maximum(got + wide, 0.0)

    def layer(mats, acts, bias, result):
        for a in range(0, along, 2):
            got = conv(mats, acts, bias, a)
            for h in range(2):
                put_shifted(result, (1 + a + h) * plane, got[:, h * LANES : (h + 1) * LANES])

    copies[2].wait()
    build_taps(w2_v, 0, chans, strip.at[0], m2, depth)
    layer([m2], [x1], bias_rows(b2, depth), x2)

    copies[3].wait()
    spread_cells(deep_v)
    for z in range(depth):
        for a in range(along):
            put_shifted(xd, (a + 1) * plane + z * SLOT, gathered(z, a))
    copies[4].wait()
    build_taps(w3_v, 0, chans, strip.at[1], m3s, depth)
    build_taps(w3_v, chans, chans, strip.at[2], m3d, depth)
    layer([m3s, m3d], [x2, xd], bias_rows(b3, depth), x3)

    copies[5].wait()
    build_taps(w4_v, 0, chans, strip.at[3], m4t, depth)
    build_taps(w4_v, chans, chans, strip.at[4], m4f, depth)
    bias = bias_rows(b4, depth)
    kinds = hw.shape[0]
    tap = hw[...].astype(F32)
    for z in range(depth):
        head[z * 4 : z * 4 + kinds, z * SLOT : z * SLOT + chans] = tap
    head_b = head[...].astype(BF)
    head_bias = column(hb, pad, 4 * depth, lambda r: r % 4)
    sz, sa = bump(depth), bump(along)
    row = lax.broadcasted_iota(jnp.int32, (4 * depth, LANES), 0)
    blend_z = jnp.full((4 * depth, LANES), float(sz[0]), F32)
    for z in range(1, depth):
        blend_z = jnp.where(row >= 4 * z, float(sz[z]), blend_z)
    across = jnp.broadcast_to(wy[...], (4 * depth, LANES))
    start = first_block[patch]
    move = offset[patch]
    for a in range(0, along, 2):
        fourth = conv([m4t, m4f], [x3, x1], bias, a).astype(BF)
        logits = jnp.dot(head_b, fourth, preferred_element_type=F32) + head_bias
        value = jax.nn.sigmoid(logits)
        for h in range(2):
            part = value[:, h * LANES : (h + 1) * LANES] * (
                blend_z * float(sa[a + h]) * across
            )
            place = move + (a + h)
            owner = lax.rem(start + place // CW, owners)
            cell = lax.rem(place, CW)
            for z in range(depth):
                for kind in range(kinds):
                    r = z * 4 + kind
                    out[z * owners + owner, kind, pl.ds(cell, 1), :] = part[r : r + 1, :]


def blend_kernel(owners, segments, first_block, mine, out):
    owner = lax.axis_index("patch")
    out[...] = jnp.zeros(out.shape, F32)
    for src in range(mine.shape[0]):
        patch = (src % owners) * segments + src // owners
        first = first_block[patch]
        ahead = lax.rem(owner - first + owners * CH_DEV, owners)
        index = jnp.minimum((first + ahead) // owners, CH_DEV - 1)
        out[index] += mine[src]


def per_device(
    features,
    deep_path,
    weight_first,
    bias_first,
    weight_second,
    bias_second,
    weight_third,
    bias_third,
    weight_fourth,
    bias_fourth,
    head_weight,
    head_bias,
    block_first,
    block_offset,
):
    segments = lax.axis_size("segment")
    owners = lax.axis_size("patch")
    count, chans, depth, along, across = features.shape
    kinds = head_weight.shape[0]
    assert count == segments and depth == segments and across == LANES
    assert along % GROUP == 0 and chans <= SLOT and depth * SLOT == LANES
    plane = depth * SLOT
    vmem = pl.BlockSpec(memory_space=pltpu.VMEM)
    smem = pl.BlockSpec(memory_space=pltpu.SMEM)
    hbm = pl.BlockSpec(memory_space=pl.ANY)
    act = pltpu.VMEM((3, (along + 2) * plane, LANES), BF)
    taps = pltpu.VMEM((plane, 9 * LANES), BF)
    wy = jnp.asarray(bump(across)).reshape(1, across)
    slots = pl.pallas_call(
        functools.partial(unet_kernel, owners),
        out_shape=jax.ShapeDtypeStruct((segments * owners, kinds, CW, across), F32),
        in_specs=[smem, smem] + [hbm] * 6 + [vmem] * 7,
        out_specs=vmem,
        scratch_shapes=[
            pltpu.VMEM((chans, depth, along, across), BF),
            pltpu.VMEM((chans, depth, along, across), BF),
            pltpu.VMEM(weight_first.shape, BF),
            pltpu.VMEM(weight_second.shape, BF),
            pltpu.VMEM(weight_third.shape, BF),
            pltpu.VMEM(weight_fourth.shape, BF),
            pltpu.VMEM((SLOT * depth * 16, LANES), F32),
            pltpu.VMEM((3, depth * (along + 2) * SLOT, LANES), BF),
            act,
            act,
            act,
            act,
            pltpu.VMEM((GROUP * SLOT, 3 * (GROUP + 2) * SLOT), F32),
            taps,
            taps,
            taps,
            taps,
            taps,
            pltpu.VMEM((5, 9, SLOT, LANES), F32),
            pltpu.VMEM((8, LANES), F32),
            pltpu.VMEM((4 * depth, LANES), F32),
            pltpu.SemaphoreType.DMA((6,)),
        ],
        compiler_params=pltpu.CompilerParams(vmem_limit_bytes=48 * 2**20),
    )(
        block_first,
        block_offset,
        features,
        deep_path,
        weight_first,
        weight_second,
        weight_third,
        weight_fourth,
        bias_first.reshape(1, chans),
        bias_second.reshape(1, chans),
        bias_third.reshape(1, chans),
        bias_fourth.reshape(1, chans),
        head_weight,
        head_bias.reshape(1, kinds),
        wy,
    )
    mine = lax.all_to_all(slots, ("segment", "patch"), split_axis=0, concat_axis=0, tiled=True)
    blended = pl.pallas_call(
        functools.partial(blend_kernel, owners, segments),
        out_shape=jax.ShapeDtypeStruct((CH_DEV, kinds, CW, across), F32),
        in_specs=[smem, vmem],
        out_specs=vmem,
    )(block_first, mine)
    return blended.reshape(CH_DEV, 1, kinds, 1, CW, across)


def solution(mesh):
    rows = P("patch", None, None, None, None)
    return jax.shard_map(
        per_device,
        mesh=mesh,
        in_specs=(rows, rows) + (P(),) * 12,
        out_specs=P(None, "patch", None, "segment", None, None),
        check_vma=False,
    )
```

```python
import functools
import math

import jax
import jax.numpy as jnp
import numpy as np
from jax import lax
from jax.experimental import pallas as pl
from jax.experimental.pallas import tpu as pltpu
from jax.sharding import PartitionSpec as P

CW = 4
CH_DEV = 8
KMAX = 4
LANES = 128
SLOT = 32
GROUP = 4
BF = jnp.bfloat16
F32 = jnp.float32


def bump(count):
    place = (np.arange(count).astype(np.float32) + np.float32(0.5)) / np.float32(count)
    return (np.sin(np.float32(np.pi) * place) ** 2).astype(np.float32)


def lane_index(rows):
    return lax.broadcasted_iota(jnp.int32, (rows, LANES), 1)


def put_shifted(act, row, value):
    rows = value.shape[0]
    lane = lane_index(rows)
    act[1, pl.ds(row, rows), :] = value.astype(BF)
    act[0, pl.ds(row, rows), :] = jnp.where(lane == 0, 0.0, pltpu.roll(value, 1, 1)).astype(BF)
    act[2, pl.ds(row, rows), :] = jnp.where(
        lane == LANES - 1, 0.0, pltpu.roll(value, LANES - 1, 1)
    ).astype(BF)


def build_taps(weight, low, chans, strip, big, depth):
    lane = lane_index(SLOT)
    for dy in range(3):
        for da in range(3):
            k = dy * 3 + da
            for dz in range(3):
                strip[k, 0:chans, dz * SLOT : dz * SLOT + chans] = weight[
                    9 * dz + 3 * da + dy, :, low : low + chans
                ].astype(F32)
            base = strip[k]
            for z in range(depth):
                shift = ((z - 1) * SLOT) % LANES
                moved = pltpu.roll(base, shift, 1) if shift else base
                if z == 0:
                    moved = jnp.where(lane < LANES - SLOT, moved, 0.0)
                if z == depth - 1:
                    moved = jnp.where(lane >= SLOT, moved, 0.0)
                big[z * SLOT : (z + 1) * SLOT, k * LANES : (k + 1) * LANES] = moved.astype(BF)


def column(row_ref, pad, rows, pick):
    pad[...] = jnp.zeros(pad.shape, F32)
    pad[0:1, 0 : row_ref.shape[1]] = row_ref[...]
    spread = jnp.broadcast_to(pad[0:1, :], (rows, LANES))
    want = pick(lax.broadcasted_iota(jnp.int32, (rows, LANES), 0))
    return jnp.sum(jnp.where(lane_index(rows) == want, spread, 0.0), axis=1, keepdims=True)


def unet_kernel(
    owners,
    first_block_h,
    offset_h,
    features,
    deep,
    w1,
    w2,
    w3,
    w4,
    b1_h,
    b2_h,
    b3_h,
    b4_h,
    hw_h,
    hb_h,
    wy_h,
    out,
    first_block,
    offset,
    feat_v,
    deep_v,
    w1_v,
    w2_v,
    w3_v,
    w4_v,
    b1,
    b2,
    b3,
    b4,
    hw,
    hb,
    wy,
    cells,
    xf,
    x1,
    x2,
    xd,
    x3,
    m1,
    m2,
    m3s,
    m3d,
    m4t,
    m4f,
    strip,
    pad,
    head,
    sems,
):
    chans, along, depth = feat_v.shape[0], feat_v.shape[1], feat_v.shape[2]
    plane = depth * SLOT
    me = lax.axis_index("segment")
    patch = lax.axis_index("patch") * features.shape[0] + me

    copies = [
        pltpu.make_async_copy(src, dst, sems.at[i])
        for i, (src, dst) in enumerate(
            [
                (features.at[me], feat_v),
                (w1, w1_v),
                (w2, w2_v),
                (deep.at[me], deep_v),
                (w3, w3_v),
                (w4, w4_v),
                (b1_h, b1),
                (b2_h, b2),
                (b3_h, b3),
                (b4_h, b4),
                (hw_h, hw),
                (hb_h, hb),
                (wy_h, wy),
                (first_block_h, first_block),
                (offset_h, offset),
            ]
        )
    ]
    for c in copies:
        c.start()

    for act in (x1, x2, xd, x3):
        for dy in range(3):
            act[dy, 0:plane, :] = jnp.zeros((plane, LANES), BF)
            act[dy, (along + 1) * plane : (along + 2) * plane, :] = jnp.zeros((plane, LANES), BF)
    high = (along + 2) * SLOT
    for dy in range(3):
        for z in range(depth):
            xf[dy, z * high : z * high + SLOT, :] = jnp.zeros((SLOT, LANES), BF)
            xf[dy, (z + 1) * high - SLOT : (z + 1) * high, :] = jnp.zeros((SLOT, LANES), BF)
    m1[...] = jnp.zeros(m1.shape, F32)
    strip[...] = jnp.zeros(strip.shape, F32)
    head[...] = jnp.zeros(head.shape, F32)
    out[...] = jnp.zeros(out.shape, F32)
    used = chans * along * depth
    cells[used:, :] = jnp.zeros((cells.shape[0] - used, LANES), F32)

    def spread_cells(source):
        for c in range(chans):
            for a in range(along):
                cells[pl.ds((c * along + a) * depth, depth), :] = source[c, a].astype(F32)

    def gathered(z, a):
        return cells[pl.ds(a * depth + z, SLOT, stride=along * depth), :]

    def own(r):
        return r

    copies[0].wait()
    spread_cells(feat_v)
    for z in range(depth):
        for a in range(along):
            put_shifted(xf, z * high + (a + 1) * SLOT, gathered(z, a))

    copies[1].wait()
    for c in copies[6:]:
        c.wait()
    span = (GROUP + 2) * SLOT
    for dy in range(3):
        for da in range(3):
            tap = w1_v[da * 3 + dy].astype(F32)
            for a in range(GROUP):
                lo = dy * span + (a + da) * SLOT
                m1[a * SLOT : a * SLOT + chans, lo : lo + chans] = tap
    m1_b = m1[...].astype(BF)

    def bias_rows(ref, copies_of):
        col = column(ref, pad, SLOT, own)
        tile = jnp.broadcast_to(col, (SLOT, LANES))
        return jnp.concatenate([tile] * copies_of, axis=0)

    bias = bias_rows(b1, GROUP)
    for z in range(depth):
        for pair in range(0, along // GROUP):
            rhs = jnp.concatenate(
                [xf[dy, pl.ds(z * high + pair * GROUP * SLOT, span), :] for dy in range(3)], axis=0
            )
            got = jnp.dot(m1_b, rhs, preferred_element_type=F32)
            got = jnp.maximum(got + bias, 0.0)
            for a in range(GROUP):
                put_shifted(
                    x1,
                    (1 + pair * GROUP + a) * plane + z * SLOT,
                    got[a * SLOT : (a + 1) * SLOT],
                )

    def window_of(act, a):
        return jnp.concatenate([act[dy, pl.ds(a * plane, 3 * plane), :] for dy in range(3)], axis=0)

    def conv(mats, acts, bias, a):
        matrix = jnp.concatenate([m[...] for m in mats], axis=1) if len(mats) > 1 else mats[0][...]
        cols = []
        for b in (a, a + 1):
            parts = [window_of(x, b) for x in acts]
            cols.append(jnp.concatenate(parts, axis=0) if len(parts) > 1 else parts[0])
        got = jnp.dot(matrix, jnp.concatenate(cols, axis=1), preferred_element_type=F32)
        wide = jnp.concatenate([bias, bias], axis=1)
        return jnp.maximum(got + wide, 0.0)

    def layer(mats, acts, bias, result):
        for a in range(0, along, 2):
            got = conv(mats, acts, bias, a)
            for h in range(2):
                put_shifted(result, (1 + a + h) * plane, got[:, h * LANES : (h + 1) * LANES])

    copies[2].wait()
    build_taps(w2_v, 0, chans, strip.at[0], m2, depth)
    layer([m2], [x1], bias_rows(b2, depth), x2)

    copies[3].wait()
    spread_cells(deep_v)
    for z in range(depth):
        for a in range(along):
            put_shifted(xd, (a + 1) * plane + z * SLOT, gathered(z, a))
    copies[4].wait()
    build_taps(w3_v, 0, chans, strip.at[1], m3s, depth)
    build_taps(w3_v, chans, chans, strip.at[2], m3d, depth)
    layer([m3s, m3d], [x2, xd], bias_rows(b3, depth), x3)

    copies[5].wait()
    build_taps(w4_v, 0, chans, strip.at[3], m4t, depth)
    build_taps(w4_v, chans, chans, strip.at[4], m4f, depth)
    bias = bias_rows(b4, depth)
    kinds = hw.shape[0]
    tap = hw[...].astype(F32)
    for z in range(depth):
        head[z * 4 : z * 4 + kinds, z * SLOT : z * SLOT + chans] = tap
    head_b = head[...].astype(BF)
    head_bias = column(hb, pad, 4 * depth, lambda r: r % 4)
    sz, sa = bump(depth), bump(along)
    row = lax.broadcasted_iota(jnp.int32, (4 * depth, LANES), 0)
    blend_z = jnp.full((4 * depth, LANES), float(sz[0]), F32)
    for z in range(1, depth):
        blend_z = jnp.where(row >= 4 * z, float(sz[z]), blend_z)
    across = jnp.broadcast_to(wy[...], (4 * depth, LANES))
    start = first_block[patch]
    move = offset[patch]
    for a in range(0, along, 2):
        fourth = conv([m4t, m4f], [x3, x1], bias, a).astype(BF)
        logits = jnp.dot(head_b, fourth, preferred_element_type=F32) + head_bias
        value = jax.nn.sigmoid(logits)
        for h in range(2):
            part = value[:, h * LANES : (h + 1) * LANES] * (
                blend_z * float(sa[a + h]) * across
            )
            place = move + (a + h)
            owner = lax.rem(start + place // CW, owners)
            cell = lax.rem(place, CW)
            for z in range(depth):
                for kind in range(kinds):
                    r = z * 4 + kind
                    out[z * owners + owner, kind, pl.ds(cell, 1), :] = part[r : r + 1, :]


def blend_kernel(owners, segments, first_block_h, mine, out, first_block, sem):
    copy = pltpu.make_async_copy(first_block_h, first_block, sem)
    copy.start()
    owner = lax.axis_index("patch")
    out[...] = jnp.zeros(out.shape, F32)
    copy.wait()
    for src in range(mine.shape[0]):
        patch = (src % owners) * segments + src // owners
        first = first_block[patch]
        ahead = lax.rem(owner - first + owners * CH_DEV, owners)
        index = jnp.minimum((first + ahead) // owners, CH_DEV - 1)
        out[index] += mine[src]


def in_hbm(*arrays):
    return [pltpu.with_memory_space_constraint(a, pltpu.HBM) for a in arrays]


def per_device(
    features,
    deep_path,
    weight_first,
    bias_first,
    weight_second,
    bias_second,
    weight_third,
    bias_third,
    weight_fourth,
    bias_fourth,
    head_weight,
    head_bias,
    block_first,
    block_offset,
):
    segments = lax.axis_size("segment")
    owners = lax.axis_size("patch")
    count, chans, depth, along, across = features.shape
    kinds = head_weight.shape[0]
    assert count == segments and depth == segments and across == LANES
    assert along % GROUP == 0 and chans <= SLOT and depth * SLOT == LANES
    plane = depth * SLOT
    vmem = pl.BlockSpec(memory_space=pltpu.VMEM)
    hbm = pl.BlockSpec(memory_space=pltpu.HBM)
    act = pltpu.VMEM((3, (along + 2) * plane, LANES), BF)
    taps = pltpu.VMEM((plane, 9 * LANES), BF)
    wy = jnp.asarray(bump(across)).reshape(1, across)
    slots = pl.pallas_call(
        functools.partial(unet_kernel, owners),
        out_shape=jax.ShapeDtypeStruct((segments * owners, kinds, CW, across), F32),
        in_specs=[hbm] * 15,
        out_specs=vmem,
        scratch_shapes=[
            pltpu.SMEM(block_first.shape, jnp.int32),
            pltpu.SMEM(block_first.shape, jnp.int32),
            pltpu.VMEM((chans, along, depth, across), BF),
            pltpu.VMEM((chans, along, depth, across), BF),
            pltpu.VMEM(weight_first.shape, BF),
            pltpu.VMEM(weight_second.shape, BF),
            pltpu.VMEM(weight_third.shape, BF),
            pltpu.VMEM(weight_fourth.shape, BF),
            pltpu.VMEM((1, chans), F32),
            pltpu.VMEM((1, chans), F32),
            pltpu.VMEM((1, chans), F32),
            pltpu.VMEM((1, chans), F32),
            pltpu.VMEM(head_weight.shape, BF),
            pltpu.VMEM((1, kinds), F32),
            pltpu.VMEM((1, across), F32),
            pltpu.VMEM((SLOT * along * depth, LANES), F32),
            pltpu.VMEM((3, depth * (along + 2) * SLOT, LANES), BF),
            act,
            act,
            act,
            act,
            pltpu.VMEM((GROUP * SLOT, 3 * (GROUP + 2) * SLOT), F32),
            taps,
            taps,
            taps,
            taps,
            taps,
            pltpu.VMEM((5, 9, SLOT, LANES), F32),
            pltpu.VMEM((8, LANES), F32),
            pltpu.VMEM((4 * depth, LANES), F32),
            pltpu.SemaphoreType.DMA((15,)),
        ],
        compiler_params=pltpu.CompilerParams(vmem_limit_bytes=48 * 2**20),
    )(
        *in_hbm(
        block_first,
        block_offset,
        features.transpose(0, 1, 3, 2, 4),
        deep_path.transpose(0, 1, 3, 2, 4),
        weight_first,
        weight_second,
        weight_third,
        weight_fourth,
        bias_first.reshape(1, chans),
        bias_second.reshape(1, chans),
        bias_third.reshape(1, chans),
        bias_fourth.reshape(1, chans),
        head_weight,
        head_bias.reshape(1, kinds),
        wy,
        )
    )
    mine = lax.all_to_all(slots, ("segment", "patch"), split_axis=0, concat_axis=0, tiled=True)
    blended = pl.pallas_call(
        functools.partial(blend_kernel, owners, segments),
        out_shape=jax.ShapeDtypeStruct((CH_DEV, kinds, CW, across), F32),
        in_specs=[hbm, vmem],
        out_specs=vmem,
        scratch_shapes=[pltpu.SMEM(block_first.shape, jnp.int32), pltpu.SemaphoreType.DMA(())],
    )(*in_hbm(block_first), mine)
    return blended.reshape(CH_DEV, 1, kinds, 1, CW, across)


def solution(mesh):
    rows = P("patch", None, None, None, None)
    return jax.shard_map(
        per_device,
        mesh=mesh,
        in_specs=(rows, rows) + (P(),) * 12,
        out_specs=P(None, "patch", None, "segment", None, None),
        check_vma=False,
    )
```

```python
import functools
import math

import jax
import jax.numpy as jnp
import numpy as np
from jax import lax
from jax.experimental import pallas as pl
from jax.experimental.pallas import tpu as pltpu
from jax.sharding import PartitionSpec as P

CW = 4
CH_DEV = 8
KMAX = 4
LANES = 128
SLOT = 32
ROWS = 16
GROUP = 4
BF = jnp.bfloat16
F32 = jnp.float32


def bump(count):
    place = (np.arange(count).astype(np.float32) + np.float32(0.5)) / np.float32(count)
    return (np.sin(np.float32(np.pi) * place) ** 2).astype(np.float32)


def lane_index(rows):
    return lax.broadcasted_iota(jnp.int32, (rows, LANES), 1)


def put_shifted(act, row, value):
    rows = value.shape[0]
    lane = lane_index(rows)
    value = value.astype(BF)
    zero = jnp.zeros(value.shape, BF)
    act[1, pl.ds(row, rows), :] = value
    act[0, pl.ds(row, rows), :] = jnp.where(lane == 0, zero, pltpu.roll(value, 1, 1))
    act[2, pl.ds(row, rows), :] = jnp.where(lane == LANES - 1, zero, pltpu.roll(value, LANES - 1, 1))


def build_block(weight, low, chans, strip, big, depth, dy, da):
    lane = lane_index(SLOT)
    zero = jnp.zeros((SLOT, LANES), BF)
    k = dy * 3 + da
    for dz in range(3):
        strip[k, 0:chans, dz * SLOT : dz * SLOT + chans] = weight[
            9 * dz + 3 * da + dy, :, low : low + chans
        ]
    base = strip[k]
    for z in range(depth):
        shift = ((z - 1) * SLOT) % LANES
        moved = pltpu.roll(base, shift, 1) if shift else base
        if z == 0:
            moved = jnp.where(lane < LANES - SLOT, moved, zero)
        if z == depth - 1:
            moved = jnp.where(lane >= SLOT, moved, zero)
        big[z * SLOT : (z + 1) * SLOT, k * LANES : (k + 1) * LANES] = moved


def column(row_ref, pad, rows, pick):
    pad[...] = jnp.zeros(pad.shape, F32)
    pad[0:1, 0 : row_ref.shape[1]] = row_ref[...]
    spread = jnp.broadcast_to(pad[0:1, :], (rows, LANES))
    want = pick(lax.broadcasted_iota(jnp.int32, (rows, LANES), 0))
    return jnp.sum(jnp.where(lane_index(rows) == want, spread, 0.0), axis=1, keepdims=True)


def unet_kernel(
    owners,
    first_block_h,
    offset_h,
    features,
    deep,
    w1,
    w2,
    w3,
    w4,
    b1_h,
    b2_h,
    b3_h,
    b4_h,
    hw_h,
    hb_h,
    wy_h,
    out,
    adder,
    first_block,
    offset,
    feat_v,
    deep_v,
    w1_v,
    w2_v,
    w3_v,
    w4_v,
    b1,
    b2,
    b3,
    b4,
    hw,
    hb,
    wy,
    cells,
    xf,
    x1,
    x2,
    xd,
    x3,
    m1,
    m2,
    m3s,
    m3d,
    m4t,
    m4f,
    strip,
    pad,
    head,
    canvas,
    sems,
):
    chans, along, depth = feat_v.shape[0], feat_v.shape[1], feat_v.shape[2]
    plane = depth * SLOT
    me = lax.axis_index("segment")
    patch = lax.axis_index("patch") * features.shape[0] + me

    copies = [
        pltpu.make_async_copy(src, dst, sems.at[i])
        for i, (src, dst) in enumerate(
            [
                (features.at[me], feat_v),
                (w1, w1_v),
                (w2, w2_v),
                (deep.at[me], deep_v),
                (w3, w3_v),
                (w4, w4_v),
                (b1_h, b1),
                (b2_h, b2),
                (b3_h, b3),
                (b4_h, b4),
                (hw_h, hw),
                (hb_h, hb),
                (wy_h, wy),
                (first_block_h, first_block),
                (offset_h, offset),
            ]
        )
    ]
    for c in copies:
        c.start()

    for act in (x1, x2, xd, x3):
        for dy in range(3):
            act[dy, 0:plane, :] = jnp.zeros((plane, LANES), BF)
            act[dy, (along + 1) * plane : (along + 2) * plane, :] = jnp.zeros((plane, LANES), BF)
    high = (along + 2) * SLOT
    for dy in range(3):
        for z in range(depth):
            xf[dy, z * high : z * high + SLOT, :] = jnp.zeros((SLOT, LANES), BF)
            xf[dy, (z + 1) * high - SLOT : (z + 1) * high, :] = jnp.zeros((SLOT, LANES), BF)
    m1[...] = jnp.zeros(m1.shape, F32)
    strip[...] = jnp.zeros(strip.shape, BF)
    head[...] = jnp.zeros(head.shape, F32)
    canvas[...] = jnp.zeros(canvas.shape, F32)
    used = chans * along * depth
    cells[used:, :] = jnp.zeros((cells.shape[0] - used, LANES), F32)

    def spread_cells(source):
        for c in range(chans):
            for a in range(along):
                cells[pl.ds((c * along + a) * depth, depth), :] = source[c, a].astype(F32)

    def gathered(z, a):
        return cells[pl.ds(a * depth + z, SLOT, stride=along * depth), :]

    def own(r):
        return r

    def make_adder():
        row = lax.broadcasted_iota(jnp.int32, (adder.shape[0], LANES), 0)
        lane = lane_index(adder.shape[0])
        here = lax.axis_index("patch")
        each = LANES // ROWS
        for block in range(adder.shape[1] // LANES):
            index = jnp.full((1, LANES), -1, jnp.int32)
            thin = lax.broadcasted_iota(jnp.int32, (1, LANES), 1)
            for j in range(each):
                src = block * each + j
                first = first_block[(src % owners) * features.shape[0] + src // owners]
                ahead = lax.rem(here - first + owners * CH_DEV, owners)
                found = jnp.where(ahead < KMAX, (first + ahead) // owners, -1)
                index = jnp.where(thin // ROWS == j, found, index)
            keep = (row // ROWS == index) & (row % ROWS == lane % ROWS)
            adder[:, block * LANES : (block + 1) * LANES] = jnp.where(keep, 1.0, 0.0).astype(BF)

    copies[0].wait()
    spread_cells(feat_v)
    for z in range(depth):
        for a in range(along):
            put_shifted(xf, z * high + (a + 1) * SLOT, gathered(z, a))

    for c in copies[1:]:
        c.wait()
    make_adder()
    span = (GROUP + 2) * SLOT
    for dy in range(3):
        for da in range(3):
            tap = w1_v[da * 3 + dy].astype(F32)
            for a in range(GROUP):
                lo = dy * span + (a + da) * SLOT
                m1[a * SLOT : a * SLOT + chans, lo : lo + chans] = tap
    m1_b = m1[...].astype(BF)

    def bias_rows(ref, copies_of):
        col = column(ref, pad, SLOT, own)
        tile = jnp.broadcast_to(col, (SLOT, LANES))
        return jnp.concatenate([tile] * copies_of, axis=0)

    def matrix_tasks(weight, low, index, big):
        return [
            functools.partial(
                build_block, weight, low, chans, strip.at[index], big, depth, dy, da
            )
            for dy in range(3)
            for da in range(3)
        ]

    def run(tasks, step, steps):
        for task in tasks[len(tasks) * step // steps : len(tasks) * (step + 1) // steps]:
            task()

    bias = bias_rows(b1, GROUP)
    bias2, bias3, bias4 = (bias_rows(b, depth) for b in (b2, b3, b4))
    tasks = matrix_tasks(w2_v, 0, 0, m2)
    for z in range(depth):
        for pair in range(0, along // GROUP):
            rhs = jnp.concatenate(
                [xf[dy, pl.ds(z * high + pair * GROUP * SLOT, span), :] for dy in range(3)], axis=0
            )
            got = jnp.dot(m1_b, rhs, preferred_element_type=F32)
            got = jnp.maximum(got + bias, 0.0)
            for a in range(GROUP):
                put_shifted(
                    x1,
                    (1 + pair * GROUP + a) * plane + z * SLOT,
                    got[a * SLOT : (a + 1) * SLOT],
                )
            run(tasks, z * (along // GROUP) + pair, depth * (along // GROUP))

    def window_of(act, a):
        return jnp.concatenate([act[dy, pl.ds(a * plane, 3 * plane), :] for dy in range(3)], axis=0)

    def conv(mats, acts, bias, a):
        matrix = jnp.concatenate([m[...] for m in mats], axis=1) if len(mats) > 1 else mats[0][...]
        cols = []
        for b in (a, a + 1):
            parts = [window_of(x, b) for x in acts]
            cols.append(jnp.concatenate(parts, axis=0) if len(parts) > 1 else parts[0])
        got = jnp.dot(matrix, jnp.concatenate(cols, axis=1), preferred_element_type=F32)
        wide = jnp.concatenate([bias, bias], axis=1)
        return jnp.maximum(got + wide, 0.0)

    def layer(mats, acts, bias, result, tasks):
        for a in range(0, along, 2):
            got = conv(mats, acts, bias, a)
            run(tasks, a // 2, along // 2)
            for h in range(2):
                put_shifted(result, (1 + a + h) * plane, got[:, h * LANES : (h + 1) * LANES])

    def deep_rows(a):
        for z in range(depth):
            put_shifted(xd, (a + 1) * plane + z * SLOT, gathered(z, a))

    spread_cells(deep_v)
    tasks = matrix_tasks(w3_v, 0, 1, m3s) + matrix_tasks(w3_v, chans, 2, m3d)
    tasks += [functools.partial(deep_rows, a) for a in range(along)]
    layer([m2], [x1], bias2, x2, tasks)
    tasks = matrix_tasks(w4_v, 0, 3, m4t) + matrix_tasks(w4_v, chans, 4, m4f)
    layer([m3s, m3d], [x2, xd], bias3, x3, tasks)
    bias = bias4
    kinds = hw.shape[0]
    tap = hw[...].astype(F32)
    for z in range(depth):
        head[z * 4 : z * 4 + kinds, z * SLOT : z * SLOT + chans] = tap
    head_b = head[...].astype(BF)
    head_bias = column(hb, pad, 4 * depth, lambda r: r % 4)
    sz, sa = bump(depth), bump(along)
    row = lax.broadcasted_iota(jnp.int32, (4 * depth, LANES), 0)
    blend_z = jnp.full((4 * depth, LANES), float(sz[0]), F32)
    for z in range(1, depth):
        blend_z = jnp.where(row >= 4 * z, float(sz[z]), blend_z)
    across = jnp.broadcast_to(wy[...], (4 * depth, LANES))
    start = first_block[patch]
    move = offset[patch]
    for a in range(0, along, 2):
        fourth = conv([m4t, m4f], [x3, x1], bias, a).astype(BF)
        logits = jnp.dot(head_b, fourth, preferred_element_type=F32) + head_bias
        value = jax.nn.sigmoid(logits)
        for h in range(2):
            part = value[:, h * LANES : (h + 1) * LANES] * (
                blend_z * float(sa[a + h]) * across
            )
            place = move + (a + h)
            owner = lax.rem(start + place // CW, owners)
            cell = lax.rem(place, CW)
            for z in range(depth):
                for kind in range(kinds):
                    r = z * 4 + kind
                    to = (z * owners + owner) * ROWS + kind * CW + cell
                    canvas[pl.ds(to, 1), :] = part[r : r + 1, :]
    for slot in range(out.shape[0]):
        out[slot] = canvas[slot * ROWS : (slot + 1) * ROWS, :].astype(BF)


def blend_kernel(adder, mine, out):
    rows = mine[...].reshape(mine.shape[0] * ROWS, LANES)
    total = jnp.dot(adder[...], rows, preferred_element_type=F32)
    for i in range(out.shape[0]):
        for kind in range(out.shape[1]):
            lo = i * ROWS + kind * CW
            out[i, kind] = total[lo : lo + CW, :]


def in_hbm(*arrays):
    return [pltpu.with_memory_space_constraint(a, pltpu.HBM) for a in arrays]


def per_device(
    features,
    deep_path,
    weight_first,
    bias_first,
    weight_second,
    bias_second,
    weight_third,
    bias_third,
    weight_fourth,
    bias_fourth,
    head_weight,
    head_bias,
    block_first,
    block_offset,
):
    segments = lax.axis_size("segment")
    owners = lax.axis_size("patch")
    count, chans, depth, along, across = features.shape
    kinds = head_weight.shape[0]
    assert count == segments and depth == segments and across == LANES
    assert along % GROUP == 0 and kinds * CW <= ROWS and chans <= SLOT and depth * SLOT == LANES
    plane = depth * SLOT
    vmem = pl.BlockSpec(memory_space=pltpu.VMEM)
    hbm = pl.BlockSpec(memory_space=pltpu.HBM)
    act = pltpu.VMEM((3, (along + 2) * plane, LANES), BF)
    taps = pltpu.VMEM((plane, 9 * LANES), BF)
    wy = jnp.asarray(bump(across)).reshape(1, across)
    slots, adder = pl.pallas_call(
        functools.partial(unet_kernel, owners),
        out_shape=(
            jax.ShapeDtypeStruct((segments * owners, ROWS, across), BF),
            jax.ShapeDtypeStruct((CH_DEV * ROWS, segments * owners * ROWS), BF),
        ),
        in_specs=[hbm] * 15,
        out_specs=(vmem, vmem),
        scratch_shapes=[
            pltpu.SMEM(block_first.shape, jnp.int32),
            pltpu.SMEM(block_first.shape, jnp.int32),
            pltpu.VMEM((chans, along, depth, across), BF),
            pltpu.VMEM((chans, along, depth, across), BF),
            pltpu.VMEM(weight_first.shape, BF),
            pltpu.VMEM(weight_second.shape, BF),
            pltpu.VMEM(weight_third.shape, BF),
            pltpu.VMEM(weight_fourth.shape, BF),
            pltpu.VMEM((1, chans), F32),
            pltpu.VMEM((1, chans), F32),
            pltpu.VMEM((1, chans), F32),
            pltpu.VMEM((1, chans), F32),
            pltpu.VMEM(head_weight.shape, BF),
            pltpu.VMEM((1, kinds), F32),
            pltpu.VMEM((1, across), F32),
            pltpu.VMEM((SLOT * along * depth, LANES), F32),
            pltpu.VMEM((3, depth * (along + 2) * SLOT, LANES), BF),
            act,
            act,
            act,
            act,
            pltpu.VMEM((GROUP * SLOT, 3 * (GROUP + 2) * SLOT), F32),
            taps,
            taps,
            taps,
            taps,
            taps,
            pltpu.VMEM((5, 9, SLOT, LANES), BF),
            pltpu.VMEM((8, LANES), F32),
            pltpu.VMEM((4 * depth, LANES), F32),
            pltpu.VMEM((segments * owners * ROWS, LANES), F32),
            pltpu.SemaphoreType.DMA((15,)),
        ],
        compiler_params=pltpu.CompilerParams(vmem_limit_bytes=48 * 2**20),
    )(
        *in_hbm(
        block_first,
        block_offset,
        features.transpose(0, 1, 3, 2, 4),
        deep_path.transpose(0, 1, 3, 2, 4),
        weight_first,
        weight_second,
        weight_third,
        weight_fourth,
        bias_first.reshape(1, chans),
        bias_second.reshape(1, chans),
        bias_third.reshape(1, chans),
        bias_fourth.reshape(1, chans),
        head_weight,
        head_bias.reshape(1, kinds),
        wy,
        )
    )
    mine = lax.all_to_all(slots, ("segment", "patch"), split_axis=0, concat_axis=0, tiled=True)
    blended = pl.pallas_call(
        blend_kernel,
        out_shape=jax.ShapeDtypeStruct((CH_DEV, kinds, CW, across), F32),
        in_specs=[vmem, vmem],
        out_specs=vmem,
    )(adder, mine)
    return blended.reshape(CH_DEV, 1, kinds, 1, CW, across)


def solution(mesh):
    rows = P("patch", None, None, None, None)
    return jax.shard_map(
        per_device,
        mesh=mesh,
        in_specs=(rows, rows) + (P(),) * 12,
        out_specs=P(None, "patch", None, "segment", None, None),
        check_vma=False,
    )
```

```python
import functools
import math

import jax
import jax.numpy as jnp
import numpy as np
from jax import lax
from jax.experimental import pallas as pl
from jax.experimental.pallas import tpu as pltpu
from jax.sharding import PartitionSpec as P

CW = 4
CH_DEV = 8
KMAX = 4
LANES = 128
SLOT = 32
ROWS = 16
GROUP = 4
BF = jnp.bfloat16
F32 = jnp.float32


def bump(count):
    place = (np.arange(count).astype(np.float32) + np.float32(0.5)) / np.float32(count)
    return (np.sin(np.float32(np.pi) * place) ** 2).astype(np.float32)


def lane_index(rows):
    return lax.broadcasted_iota(jnp.int32, (rows, LANES), 1)


def put_shifted(act, row, value):
    rows = value.shape[0]
    lane = lane_index(rows)
    value = value.astype(BF)
    zero = jnp.zeros(value.shape, BF)
    act[1, pl.ds(row, rows), :] = value
    act[0, pl.ds(row, rows), :] = jnp.where(lane == 0, zero, pltpu.roll(value, 1, 1))
    act[2, pl.ds(row, rows), :] = jnp.where(lane == LANES - 1, zero, pltpu.roll(value, LANES - 1, 1))


def build_block(weight, low, chans, strip, big, depth, dy, da):
    lane = lane_index(SLOT)
    zero = jnp.zeros((SLOT, LANES), BF)
    k = dy * 3 + da
    for dz in range(3):
        strip[k, 0:chans, dz * SLOT : dz * SLOT + chans] = weight[
            9 * dz + 3 * da + dy, :, low : low + chans
        ]
    base = strip[k]
    for z in range(depth):
        shift = ((z - 1) * SLOT) % LANES
        moved = pltpu.roll(base, shift, 1) if shift else base
        if z == 0:
            moved = jnp.where(lane < LANES - SLOT, moved, zero)
        if z == depth - 1:
            moved = jnp.where(lane >= SLOT, moved, zero)
        big[z * SLOT : (z + 1) * SLOT, k * LANES : (k + 1) * LANES] = moved


def column(row_ref, pad, rows, pick):
    pad[...] = jnp.zeros(pad.shape, F32)
    pad[0:1, 0 : row_ref.shape[1]] = row_ref[...]
    spread = jnp.broadcast_to(pad[0:1, :], (rows, LANES))
    want = pick(lax.broadcasted_iota(jnp.int32, (rows, LANES), 0))
    return jnp.sum(jnp.where(lane_index(rows) == want, spread, 0.0), axis=1, keepdims=True)


def unet_kernel(
    owners,
    first_block_h,
    offset_h,
    features,
    deep,
    w1,
    w2,
    w3,
    w4,
    b1_h,
    b2_h,
    b3_h,
    b4_h,
    hw_h,
    hb_h,
    wy_h,
    out,
    adder,
    first_block,
    offset,
    feat_v,
    deep_v,
    w1_v,
    w2_v,
    w3_v,
    w4_v,
    b1,
    b2,
    b3,
    b4,
    hw,
    hb,
    wy,
    cells,
    xf,
    x1,
    x2,
    xd,
    x3,
    m1,
    m2,
    m3s,
    m3d,
    m4t,
    m4f,
    strip,
    pad,
    head,
    canvas,
    sems,
):
    chans, along, depth = feat_v.shape[0], feat_v.shape[1], feat_v.shape[2]
    plane = depth * SLOT
    me = lax.axis_index("segment")
    patch = lax.axis_index("patch") * features.shape[0] + me

    copies = [
        pltpu.make_async_copy(src, dst, sems.at[i])
        for i, (src, dst) in enumerate(
            [
                (features.at[me], feat_v),
                (w1, w1_v),
                (w2, w2_v),
                (deep.at[me], deep_v),
                (w3, w3_v),
                (w4, w4_v),
                (b1_h, b1),
                (b2_h, b2),
                (b3_h, b3),
                (b4_h, b4),
                (hw_h, hw),
                (hb_h, hb),
                (wy_h, wy),
                (first_block_h, first_block),
                (offset_h, offset),
            ]
        )
    ]
    for c in copies:
        c.start()

    for act in (x1, x2, xd, x3):
        for dy in range(3):
            act[dy, 0:plane, :] = jnp.zeros((plane, LANES), BF)
            act[dy, (along + 1) * plane : (along + 2) * plane, :] = jnp.zeros((plane, LANES), BF)
    high = (along + 2) * SLOT
    for dy in range(3):
        for z in range(depth):
            xf[dy, z * high : z * high + SLOT, :] = jnp.zeros((SLOT, LANES), BF)
            xf[dy, (z + 1) * high - SLOT : (z + 1) * high, :] = jnp.zeros((SLOT, LANES), BF)
    m1[...] = jnp.zeros(m1.shape, F32)
    strip[...] = jnp.zeros(strip.shape, BF)
    head[...] = jnp.zeros(head.shape, F32)
    canvas[...] = jnp.zeros(canvas.shape, F32)
    used = chans * along * depth
    cells[used:, :] = jnp.zeros((cells.shape[0] - used, LANES), F32)

    def spread_cells(source):
        for c in range(chans):
            for a in range(along):
                cells[pl.ds((c * along + a) * depth, depth), :] = source[c, a].astype(F32)

    def gathered(z, a):
        return cells[pl.ds(a * depth + z, SLOT, stride=along * depth), :]

    def own(r):
        return r

    def make_adder():
        row = lax.broadcasted_iota(jnp.int32, (adder.shape[0], LANES), 0)
        lane = lane_index(adder.shape[0])
        here = lax.axis_index("patch")
        each = LANES // ROWS
        for block in range(adder.shape[1] // LANES):
            index = jnp.full((1, LANES), -1, jnp.int32)
            thin = lax.broadcasted_iota(jnp.int32, (1, LANES), 1)
            for j in range(each):
                src = block * each + j
                first = first_block[(src % owners) * features.shape[0] + src // owners]
                ahead = lax.rem(here - first + owners * CH_DEV, owners)
                found = jnp.where(ahead < KMAX, (first + ahead) // owners, -1)
                index = jnp.where(thin // ROWS == j, found, index)
            keep = (row // ROWS == index) & (row % ROWS == lane % ROWS)
            adder[:, block * LANES : (block + 1) * LANES] = jnp.where(keep, 1.0, 0.0).astype(BF)

    copies[0].wait()
    spread_cells(feat_v)
    for z in range(depth):
        for a in range(along):
            put_shifted(xf, z * high + (a + 1) * SLOT, gathered(z, a))

    for c in copies[1:]:
        c.wait()
    make_adder()
    span = (GROUP + 2) * SLOT
    for dy in range(3):
        for da in range(3):
            tap = w1_v[da * 3 + dy].astype(F32)
            for a in range(GROUP):
                lo = dy * span + (a + da) * SLOT
                m1[a * SLOT : a * SLOT + chans, lo : lo + chans] = tap
    m1_b = m1[...].astype(BF)

    def bias_rows(ref, copies_of):
        col = column(ref, pad, SLOT, own)
        tile = jnp.broadcast_to(col, (SLOT, LANES))
        return jnp.concatenate([tile] * copies_of, axis=0)

    def matrix_tasks(weight, low, index, big):
        return [
            functools.partial(
                build_block, weight, low, chans, strip.at[index], big, depth, dy, da
            )
            for dy in range(3)
            for da in range(3)
        ]

    def run(tasks, step, steps):
        for task in tasks[len(tasks) * step // steps : len(tasks) * (step + 1) // steps]:
            task()

    bias = bias_rows(b1, GROUP)
    bias2, bias3, bias4 = (bias_rows(b, depth) for b in (b2, b3, b4))
    tasks = matrix_tasks(w2_v, 0, 0, m2)
    for z in range(depth):
        for pair in range(0, along // GROUP):
            rhs = jnp.concatenate(
                [xf[dy, pl.ds(z * high + pair * GROUP * SLOT, span), :] for dy in range(3)], axis=0
            )
            got = jnp.dot(m1_b, rhs, preferred_element_type=F32)
            got = jnp.maximum(got + bias, 0.0)
            for a in range(GROUP):
                put_shifted(
                    x1,
                    (1 + pair * GROUP + a) * plane + z * SLOT,
                    got[a * SLOT : (a + 1) * SLOT],
                )
            run(tasks, z * (along // GROUP) + pair, depth * (along // GROUP))

    def window_of(act, a):
        return jnp.concatenate([act[dy, pl.ds(a * plane, 3 * plane), :] for dy in range(3)], axis=0)

    def conv(mats, acts, bias, a):
        matrix = jnp.concatenate([m[...] for m in mats], axis=1) if len(mats) > 1 else mats[0][...]
        cols = []
        for b in (a, a + 1):
            parts = [window_of(x, b) for x in acts]
            cols.append(jnp.concatenate(parts, axis=0) if len(parts) > 1 else parts[0])
        got = jnp.dot(matrix, jnp.concatenate(cols, axis=1), preferred_element_type=F32)
        wide = jnp.concatenate([bias, bias], axis=1)
        return jnp.maximum(got + wide, 0.0)

    def layer(mats, acts, bias, result, tasks):
        for a in range(0, along, 2):
            got = conv(mats, acts, bias, a)
            run(tasks, a // 2, along // 2)
            for h in range(2):
                put_shifted(result, (1 + a + h) * plane, got[:, h * LANES : (h + 1) * LANES])

    def deep_rows(a):
        for z in range(depth):
            put_shifted(xd, (a + 1) * plane + z * SLOT, gathered(z, a))

    spread_cells(deep_v)
    tasks = matrix_tasks(w3_v, 0, 1, m3s) + matrix_tasks(w3_v, chans, 2, m3d)
    tasks += [functools.partial(deep_rows, a) for a in range(along)]
    layer([m2], [x1], bias2, x2, tasks)
    tasks = matrix_tasks(w4_v, 0, 3, m4t) + matrix_tasks(w4_v, chans, 4, m4f)
    layer([m3s, m3d], [x2, xd], bias3, x3, tasks)
    bias = bias4
    kinds = hw.shape[0]
    tap = hw[...].astype(F32)
    for z in range(depth):
        head[z * 4 : z * 4 + kinds, z * SLOT : z * SLOT + chans] = tap
    head_b = head[...].astype(BF)
    head_bias = column(hb, pad, 4 * depth, lambda r: r % 4)
    sz, sa = bump(depth), bump(along)
    row = lax.broadcasted_iota(jnp.int32, (4 * depth, LANES), 0)
    blend_z = jnp.full((4 * depth, LANES), float(sz[0]), F32)
    for z in range(1, depth):
        blend_z = jnp.where(row >= 4 * z, float(sz[z]), blend_z)
    across = jnp.broadcast_to(wy[...], (4 * depth, LANES))
    start = first_block[patch]
    move = offset[patch]
    for a in range(0, along, 2):
        fourth = conv([m4t, m4f], [x3, x1], bias, a).astype(BF)
        logits = jnp.dot(head_b, fourth, preferred_element_type=F32) + head_bias
        value = jax.nn.sigmoid(logits)
        for h in range(2):
            part = value[:, h * LANES : (h + 1) * LANES] * (
                blend_z * float(sa[a + h]) * across
            )
            place = move + (a + h)
            owner = lax.rem(start + place // CW, owners)
            cell = lax.rem(place, CW)
            for z in range(depth):
                for kind in range(kinds):
                    r = z * 4 + kind
                    to = (z * owners + owner) * ROWS + kind * CW + cell
                    canvas[pl.ds(to, 1), :] = part[r : r + 1, :]
    for slot in range(out.shape[0]):
        out[slot] = canvas[slot * ROWS : (slot + 1) * ROWS, :].astype(BF)


def blend_kernel(adder, mine, out):
    rows = mine[...].reshape(mine.shape[0] * ROWS, LANES)
    total = jnp.dot(adder[...], rows, preferred_element_type=F32)
    for i in range(out.shape[0]):
        for kind in range(out.shape[1]):
            lo = i * ROWS + kind * CW
            out[i, kind] = total[lo : lo + CW, :]


def held_in(space, *arrays):
    return [pltpu.with_memory_space_constraint(a, space) for a in arrays]


def per_device(
    features,
    deep_path,
    weight_first,
    bias_first,
    weight_second,
    bias_second,
    weight_third,
    bias_third,
    weight_fourth,
    bias_fourth,
    head_weight,
    head_bias,
    block_first,
    block_offset,
):
    segments = lax.axis_size("segment")
    owners = lax.axis_size("patch")
    count, chans, depth, along, across = features.shape
    kinds = head_weight.shape[0]
    assert count == segments and depth == segments and across == LANES
    assert along % GROUP == 0 and kinds * CW <= ROWS and chans <= SLOT and depth * SLOT == LANES
    plane = depth * SLOT
    vmem = pl.BlockSpec(memory_space=pltpu.VMEM)
    hbm = pl.BlockSpec(memory_space=pltpu.HBM)
    act = pltpu.VMEM((3, (along + 2) * plane, LANES), BF)
    taps = pltpu.VMEM((plane, 9 * LANES), BF)
    wy = jnp.asarray(bump(across)).reshape(1, across)
    slots, adder = pl.pallas_call(
        functools.partial(unet_kernel, owners),
        out_shape=(
            jax.ShapeDtypeStruct((segments * owners, ROWS, across), BF),
            jax.ShapeDtypeStruct((CH_DEV * ROWS, segments * owners * ROWS), BF),
        ),
        in_specs=[hbm] * 15,
        out_specs=(vmem, vmem),
        scratch_shapes=[
            pltpu.SMEM(block_first.shape, jnp.int32),
            pltpu.SMEM(block_first.shape, jnp.int32),
            pltpu.VMEM((chans, along, depth, across), BF),
            pltpu.VMEM((chans, along, depth, across), BF),
            pltpu.VMEM(weight_first.shape, BF),
            pltpu.VMEM(weight_second.shape, BF),
            pltpu.VMEM(weight_third.shape, BF),
            pltpu.VMEM(weight_fourth.shape, BF),
            pltpu.VMEM((1, chans), F32),
            pltpu.VMEM((1, chans), F32),
            pltpu.VMEM((1, chans), F32),
            pltpu.VMEM((1, chans), F32),
            pltpu.VMEM(head_weight.shape, BF),
            pltpu.VMEM((1, kinds), F32),
            pltpu.VMEM((1, across), F32),
            pltpu.VMEM((SLOT * along * depth, LANES), F32),
            pltpu.VMEM((3, depth * (along + 2) * SLOT, LANES), BF),
            act,
            act,
            act,
            act,
            pltpu.VMEM((GROUP * SLOT, 3 * (GROUP + 2) * SLOT), F32),
            taps,
            taps,
            taps,
            taps,
            taps,
            pltpu.VMEM((5, 9, SLOT, LANES), BF),
            pltpu.VMEM((8, LANES), F32),
            pltpu.VMEM((4 * depth, LANES), F32),
            pltpu.VMEM((segments * owners * ROWS, LANES), F32),
            pltpu.SemaphoreType.DMA((15,)),
        ],
        compiler_params=pltpu.CompilerParams(vmem_limit_bytes=48 * 2**20),
    )(
        *held_in(
            pltpu.HBM,
        block_first,
        block_offset,
        features.transpose(0, 1, 3, 2, 4),
        deep_path.transpose(0, 1, 3, 2, 4),
        weight_first,
        weight_second,
        weight_third,
        weight_fourth,
        bias_first.reshape(1, chans),
        bias_second.reshape(1, chans),
        bias_third.reshape(1, chans),
        bias_fourth.reshape(1, chans),
        head_weight,
        head_bias.reshape(1, kinds),
        wy,
        )
    )
    mine = lax.all_to_all(slots, ("segment", "patch"), split_axis=0, concat_axis=0, tiled=True)
    blended = pl.pallas_call(
        blend_kernel,
        out_shape=jax.ShapeDtypeStruct((CH_DEV, kinds, CW, across), F32),
        in_specs=[vmem, vmem],
        out_specs=vmem,
    )(*held_in(pltpu.VMEM, adder, mine))
    return blended.reshape(CH_DEV, 1, kinds, 1, CW, across)


def solution(mesh):
    rows = P("patch", None, None, None, None)
    return jax.shard_map(
        per_device,
        mesh=mesh,
        in_specs=(rows, rows) + (P(),) * 12,
        out_specs=P(None, "patch", None, "segment", None, None),
        check_vma=False,
    )
```

```python
import functools
import math

import jax
import jax.numpy as jnp
import numpy as np
from jax import lax
from jax.experimental import pallas as pl
from jax.experimental.pallas import tpu as pltpu
from jax.sharding import PartitionSpec as P

CW = 4
CH_DEV = 8
KMAX = 4
LANES = 128
SLOT = 32
TILE = 16
ROWS = 16
GROUP = 4
BF = jnp.bfloat16
F32 = jnp.float32


def bump(count):
    place = (np.arange(count).astype(np.float32) + np.float32(0.5)) / np.float32(count)
    return (np.sin(np.float32(np.pi) * place) ** 2).astype(np.float32)


def lane_index(rows):
    return lax.broadcasted_iota(jnp.int32, (rows, LANES), 1)


def lane_mask(low, high):
    lane = lane_index(TILE)
    return jnp.where((lane >= low) & (lane < high), 1.0, 0.0).astype(BF)


def masked(value, tile):
    rows = value.shape[0]
    return (value.reshape(rows // TILE, TILE, LANES) * tile[None]).reshape(rows, LANES)


def put_shifted(act, row, value):
    rows = value.shape[0]
    value = value.astype(BF)
    act[1, pl.ds(row, rows), :] = value
    act[0, pl.ds(row, rows), :] = masked(pltpu.roll(value, 1, 1), lane_mask(1, LANES))
    act[2, pl.ds(row, rows), :] = masked(
        pltpu.roll(value, LANES - 1, 1), lane_mask(0, LANES - 1)
    )


def turned(value, lanes):
    return pltpu.roll(value, lanes % LANES, 1) if lanes % LANES else value


def pad_taps(weight, padded):
    taps, rows, cols = weight.shape
    for t in range(taps):
        padded[t, 0:rows, 0:cols] = weight[t]


def build_bands(padded, low, chans, wide, big, depth, da):
    parts = []
    for dz in range(3):
        taps = padded[9 * dz + 3 * da : 9 * dz + 3 * da + 3].reshape(3 * SLOT, LANES)
        if low or wide:
            taps = masked(taps, lane_mask(low, low + chans))
        parts.append(turned(taps, dz * SLOT - low))
    base = parts[0] + parts[1] + parts[2]
    for z in range(depth):
        moved = turned(base, (z - 1) * SLOT)
        if z == 0:
            moved = masked(moved, lane_mask(0, LANES - SLOT))
        if z == depth - 1:
            moved = masked(moved, lane_mask(SLOT, LANES))
        for dy in range(3):
            k = da * 3 + dy
            big[z * SLOT : (z + 1) * SLOT, k * LANES : (k + 1) * LANES] = moved[
                dy * SLOT : (dy + 1) * SLOT
            ]


def build_first(padded, big):
    parts = [padded[3 * da : 3 * da + 3].reshape(3 * SLOT, LANES) for da in range(3)]
    base = parts[0] + turned(parts[1], SLOT) + turned(parts[2], 2 * SLOT)
    for a in range(GROUP):
        moved = turned(base, a * SLOT)
        wide = masked(moved, lane_mask(a * SLOT, LANES))
        rest = masked(moved, lane_mask(0, (a - 1) * SLOT))
        rows = slice(a * SLOT, (a + 1) * SLOT)
        for dy in range(3):
            big[rows, dy * LANES : (dy + 1) * LANES] = wide[dy * SLOT : (dy + 1) * SLOT]
        half = [rest[dy * SLOT : (dy + 1) * SLOT] for dy in range(3)]
        big[rows, 3 * LANES : 4 * LANES] = half[0] + turned(half[1], LANES // 2)
        big[rows, 4 * LANES : 5 * LANES] = half[2]


def column(row_ref, pad, rows, pick):
    pad[...] = jnp.zeros(pad.shape, F32)
    pad[0:1, 0 : row_ref.shape[1]] = row_ref[...]
    spread = jnp.broadcast_to(pad[0:1, :], (rows, LANES))
    want = pick(lax.broadcasted_iota(jnp.int32, (rows, LANES), 0))
    return jnp.sum(jnp.where(lane_index(rows) == want, spread, 0.0), axis=1, keepdims=True)


def unet_kernel(
    owners,
    first_block_h,
    offset_h,
    features,
    deep,
    w1,
    w2,
    w3,
    w4,
    b1_h,
    b2_h,
    b3_h,
    b4_h,
    hw_h,
    hb_h,
    wy_h,
    out,
    adder,
    first_block,
    offset,
    feat_v,
    deep_v,
    w1_v,
    w2_v,
    w3_v,
    w4_v,
    b1,
    b2,
    b3,
    b4,
    hw,
    hb,
    wy,
    cells,
    xf,
    x1,
    x2,
    xd,
    x3,
    m1,
    m2,
    m3s,
    m3d,
    m4t,
    m4f,
    p1,
    p2,
    p3,
    p4,
    pad,
    head,
    canvas,
    sems,
):
    chans, along, depth = feat_v.shape[0], feat_v.shape[1], feat_v.shape[2]
    plane = depth * SLOT
    me = lax.axis_index("segment")
    patch = lax.axis_index("patch") * features.shape[0] + me

    copies = [
        pltpu.make_async_copy(src, dst, sems.at[i])
        for i, (src, dst) in enumerate(
            [
                (features.at[me], feat_v),
                (w1, w1_v),
                (w2, w2_v),
                (deep.at[me], deep_v),
                (w3, w3_v),
                (w4, w4_v),
                (b1_h, b1),
                (b2_h, b2),
                (b3_h, b3),
                (b4_h, b4),
                (hw_h, hw),
                (hb_h, hb),
                (wy_h, wy),
                (first_block_h, first_block),
                (offset_h, offset),
            ]
        )
    ]
    for c in copies:
        c.start()

    for act in (x1, x2, xd, x3):
        for dy in range(3):
            act[dy, 0:plane, :] = jnp.zeros((plane, LANES), BF)
            act[dy, (along + 1) * plane : (along + 2) * plane, :] = jnp.zeros((plane, LANES), BF)
    high = (along + 2) * SLOT
    for dy in range(3):
        for z in range(depth):
            xf[dy, z * high : z * high + SLOT, :] = jnp.zeros((SLOT, LANES), BF)
            xf[dy, (z + 1) * high - SLOT : (z + 1) * high, :] = jnp.zeros((SLOT, LANES), BF)
    for padded in (p1, p2, p3, p4):
        padded[...] = jnp.zeros(padded.shape, BF)
    head[...] = jnp.zeros(head.shape, F32)
    canvas[...] = jnp.zeros(canvas.shape, F32)
    used = chans * along * depth
    cells[used:, :] = jnp.zeros((cells.shape[0] - used, LANES), F32)

    def spread_cells(source):
        for c in range(chans):
            for a in range(along):
                cells[pl.ds((c * along + a) * depth, depth), :] = source[c, a].astype(F32)

    def gathered(z, a):
        return cells[pl.ds(a * depth + z, SLOT, stride=along * depth), :]

    def own(r):
        return r

    def make_adder():
        row = lax.broadcasted_iota(jnp.int32, (adder.shape[0], LANES), 0)
        lane = lane_index(adder.shape[0])
        here = lax.axis_index("patch")
        each = LANES // ROWS
        for block in range(adder.shape[1] // LANES):
            index = jnp.full((1, LANES), -1, jnp.int32)
            thin = lax.broadcasted_iota(jnp.int32, (1, LANES), 1)
            for j in range(each):
                src = block * each + j
                first = first_block[(src % owners) * features.shape[0] + src // owners]
                ahead = lax.rem(here - first + owners * CH_DEV, owners)
                found = jnp.where(ahead < KMAX, (first + ahead) // owners, -1)
                index = jnp.where(thin // ROWS == j, found, index)
            keep = (row // ROWS == index) & (row % ROWS == lane % ROWS)
            adder[:, block * LANES : (block + 1) * LANES] = jnp.where(keep, 1.0, 0.0).astype(BF)

    copies[0].wait()
    spread_cells(feat_v)
    for z in range(depth):
        for a in range(along):
            put_shifted(xf, z * high + (a + 1) * SLOT, gathered(z, a))

    copies[1].wait()
    pad_taps(w1_v, p1)
    build_first(p1, m1)
    for c in copies[2:]:
        c.wait()
    make_adder()
    for weight, padded in ((w2_v, p2), (w3_v, p3), (w4_v, p4)):
        pad_taps(weight, padded)

    def bias_rows(ref, copies_of):
        col = column(ref, pad, SLOT, own)
        tile = jnp.broadcast_to(col, (SLOT, LANES))
        return jnp.concatenate([tile] * copies_of, axis=0)

    def matrix_tasks(padded, low, wide, big):
        return [
            functools.partial(build_bands, padded, low, chans, wide, big, depth, da)
            for da in range(3)
        ]

    def run(tasks, step, steps):
        for task in tasks[len(tasks) * step // steps : len(tasks) * (step + 1) // steps]:
            task()

    bias = bias_rows(b1, GROUP)
    bias2, bias3, bias4 = (bias_rows(b, depth) for b in (b2, b3, b4))
    tasks = matrix_tasks(p2, 0, False, m2)
    columns = [(z, group) for z in range(depth) for group in range(along // GROUP)]

    def first_window(z, group):
        low = z * high + group * GROUP * SLOT
        pieces = [xf[dy, pl.ds(low, LANES), :] for dy in range(3)]
        pieces += [xf[dy, pl.ds(low + LANES, LANES // 2), :] for dy in range(3)]
        return jnp.concatenate(pieces, axis=0)

    for pair in range(0, len(columns), 2):
        rhs = jnp.concatenate([first_window(*c) for c in columns[pair : pair + 2]], axis=1)
        got = jnp.dot(m1[:, 0 : rhs.shape[0]], rhs, preferred_element_type=F32)
        run(tasks, pair // 2, len(columns) // 2)
        for h, (z, group) in enumerate(columns[pair : pair + 2]):
            part = jnp.maximum(got[:, h * LANES : (h + 1) * LANES] + bias, 0.0)
            for a in range(GROUP):
                put_shifted(
                    x1,
                    (1 + group * GROUP + a) * plane + z * SLOT,
                    part[a * SLOT : (a + 1) * SLOT],
                )

    def window_of(act, a):
        return jnp.concatenate(
            [act[dy, pl.ds((a + da) * plane, plane), :] for da in range(3) for dy in range(3)],
            axis=0,
        )

    def conv(mats, acts, bias, a):
        matrix = jnp.concatenate([m[...] for m in mats], axis=1) if len(mats) > 1 else mats[0][...]
        cols = []
        for b in (a, a + 1):
            parts = [window_of(x, b) for x in acts]
            cols.append(jnp.concatenate(parts, axis=0) if len(parts) > 1 else parts[0])
        got = jnp.dot(matrix, jnp.concatenate(cols, axis=1), preferred_element_type=F32)
        wide = jnp.concatenate([bias, bias], axis=1)
        return jnp.maximum(got + wide, 0.0)

    def layer(mats, acts, bias, result, tasks):
        for a in range(0, along, 2):
            got = conv(mats, acts, bias, a)
            run(tasks, a // 2, along // 2)
            for h in range(2):
                put_shifted(result, (1 + a + h) * plane, got[:, h * LANES : (h + 1) * LANES])

    def deep_rows(a):
        for z in range(depth):
            put_shifted(xd, (a + 1) * plane + z * SLOT, gathered(z, a))

    spread_cells(deep_v)
    tasks = matrix_tasks(p3, 0, True, m3s) + matrix_tasks(p3, chans, True, m3d)
    tasks += [functools.partial(deep_rows, a) for a in range(along)]
    layer([m2], [x1], bias2, x2, tasks)
    tasks = matrix_tasks(p4, 0, True, m4t) + matrix_tasks(p4, chans, True, m4f)
    layer([m3s, m3d], [x2, xd], bias3, x3, tasks)
    bias = bias4
    kinds = hw.shape[0]
    tap = hw[...].astype(F32)
    for z in range(depth):
        head[z * 4 : z * 4 + kinds, z * SLOT : z * SLOT + chans] = tap
    head_b = head[...].astype(BF)
    head_bias = column(hb, pad, 4 * depth, lambda r: r % 4)
    sz, sa = bump(depth), bump(along)
    row = lax.broadcasted_iota(jnp.int32, (4 * depth, LANES), 0)
    blend_z = jnp.full((4 * depth, LANES), float(sz[0]), F32)
    for z in range(1, depth):
        blend_z = jnp.where(row >= 4 * z, float(sz[z]), blend_z)
    across = jnp.broadcast_to(wy[...], (4 * depth, LANES))
    start = first_block[patch]
    move = offset[patch]
    for a in range(0, along, 2):
        fourth = conv([m4t, m4f], [x3, x1], bias, a).astype(BF)
        logits = jnp.dot(head_b, fourth, preferred_element_type=F32) + head_bias
        value = jax.nn.sigmoid(logits)
        for h in range(2):
            part = value[:, h * LANES : (h + 1) * LANES] * (
                blend_z * float(sa[a + h]) * across
            )
            place = move + (a + h)
            owner = lax.rem(start + place // CW, owners)
            cell = lax.rem(place, CW)
            for z in range(depth):
                for kind in range(kinds):
                    r = z * 4 + kind
                    to = (z * owners + owner) * ROWS + kind * CW + cell
                    canvas[pl.ds(to, 1), :] = part[r : r + 1, :]
    for slot in range(out.shape[0]):
        out[slot] = canvas[slot * ROWS : (slot + 1) * ROWS, :].astype(BF)


def blend_kernel(adder, mine, out):
    rows = mine[...].reshape(mine.shape[0] * ROWS, LANES)
    total = jnp.dot(adder[...], rows, preferred_element_type=F32)
    for i in range(out.shape[0]):
        for kind in range(out.shape[1]):
            lo = i * ROWS + kind * CW
            out[i, kind] = total[lo : lo + CW, :]


def held_in(space, *arrays):
    return [pltpu.with_memory_space_constraint(a, space) for a in arrays]


def per_device(
    features,
    deep_path,
    weight_first,
    bias_first,
    weight_second,
    bias_second,
    weight_third,
    bias_third,
    weight_fourth,
    bias_fourth,
    head_weight,
    head_bias,
    block_first,
    block_offset,
):
    segments = lax.axis_size("segment")
    owners = lax.axis_size("patch")
    count, chans, depth, along, across = features.shape
    kinds = head_weight.shape[0]
    assert count == segments and depth == segments and across == LANES
    assert along % GROUP == 0 and kinds * CW <= ROWS and chans <= SLOT and depth * SLOT == LANES
    plane = depth * SLOT
    vmem = pl.BlockSpec(memory_space=pltpu.VMEM)
    hbm = pl.BlockSpec(memory_space=pltpu.HBM)
    act = pltpu.VMEM((3, (along + 2) * plane, LANES), BF)
    taps = pltpu.VMEM((plane, 9 * LANES), BF)
    wy = jnp.asarray(bump(across)).reshape(1, across)
    slots, adder = pl.pallas_call(
        functools.partial(unet_kernel, owners),
        out_shape=(
            jax.ShapeDtypeStruct((segments * owners, ROWS, across), BF),
            jax.ShapeDtypeStruct((CH_DEV * ROWS, segments * owners * ROWS), BF),
        ),
        in_specs=[hbm] * 15,
        out_specs=(vmem, vmem),
        scratch_shapes=[
            pltpu.SMEM(block_first.shape, jnp.int32),
            pltpu.SMEM(block_first.shape, jnp.int32),
            pltpu.VMEM((chans, along, depth, across), BF),
            pltpu.VMEM((chans, along, depth, across), BF),
            pltpu.VMEM(weight_first.shape, BF),
            pltpu.VMEM(weight_second.shape, BF),
            pltpu.VMEM(weight_third.shape, BF),
            pltpu.VMEM(weight_fourth.shape, BF),
            pltpu.VMEM((1, chans), F32),
            pltpu.VMEM((1, chans), F32),
            pltpu.VMEM((1, chans), F32),
            pltpu.VMEM((1, chans), F32),
            pltpu.VMEM(head_weight.shape, BF),
            pltpu.VMEM((1, kinds), F32),
            pltpu.VMEM((1, across), F32),
            pltpu.VMEM((SLOT * along * depth, LANES), F32),
            pltpu.VMEM((3, depth * (along + 2) * SLOT, LANES), BF),
            act,
            act,
            act,
            act,
            pltpu.VMEM((GROUP * SLOT, 5 * LANES), BF),
            taps,
            taps,
            taps,
            taps,
            taps,
            pltpu.VMEM((9, SLOT, LANES), BF),
            pltpu.VMEM((27, SLOT, LANES), BF),
            pltpu.VMEM((27, SLOT, LANES), BF),
            pltpu.VMEM((27, SLOT, LANES), BF),
            pltpu.VMEM((8, LANES), F32),
            pltpu.VMEM((4 * depth, LANES), F32),
            pltpu.VMEM((segments * owners * ROWS, LANES), F32),
            pltpu.SemaphoreType.DMA((15,)),
        ],
        compiler_params=pltpu.CompilerParams(vmem_limit_bytes=48 * 2**20),
    )(
        *held_in(
            pltpu.HBM,
        block_first,
        block_offset,
        features.transpose(0, 1, 3, 2, 4),
        deep_path.transpose(0, 1, 3, 2, 4),
        weight_first,
        weight_second,
        weight_third,
        weight_fourth,
        bias_first.reshape(1, chans),
        bias_second.reshape(1, chans),
        bias_third.reshape(1, chans),
        bias_fourth.reshape(1, chans),
        head_weight,
        head_bias.reshape(1, kinds),
        wy,
        )
    )
    mine = lax.all_to_all(slots, ("segment", "patch"), split_axis=0, concat_axis=0, tiled=True)
    blended = pl.pallas_call(
        blend_kernel,
        out_shape=jax.ShapeDtypeStruct((CH_DEV, kinds, CW, across), F32),
        in_specs=[vmem, vmem],
        out_specs=vmem,
    )(*held_in(pltpu.VMEM, adder, mine))
    return blended.reshape(CH_DEV, 1, kinds, 1, CW, across)


def solution(mesh):
    rows = P("patch", None, None, None, None)
    return jax.shard_map(
        per_device,
        mesh=mesh,
        in_specs=(rows, rows) + (P(),) * 12,
        out_specs=P(None, "patch", None, "segment", None, None),
        check_vma=False,
    )
```

```python
import functools
import math

import jax
import jax.numpy as jnp
import numpy as np
from jax import lax
from jax.experimental import pallas as pl
from jax.experimental.pallas import tpu as pltpu
from jax.sharding import PartitionSpec as P

CW = 4
CH_DEV = 8
KMAX = 4
LANES = 128
SLOT = 32
TILE = 16
ROWS = 16
GROUP = 4
BF = jnp.bfloat16
F32 = jnp.float32


def bump(count):
    place = (np.arange(count).astype(np.float32) + np.float32(0.5)) / np.float32(count)
    return (np.sin(np.float32(np.pi) * place) ** 2).astype(np.float32)


def lane_index(rows):
    return lax.broadcasted_iota(jnp.int32, (rows, LANES), 1)


def lane_mask(low, high):
    lane = lane_index(TILE)
    return jnp.where((lane >= low) & (lane < high), 1.0, 0.0).astype(BF)


def masked(value, tile):
    rows = value.shape[0]
    return (value.reshape(rows // TILE, TILE, LANES) * tile[None]).reshape(rows, LANES)


def put_shifted(act, row, value):
    rows = value.shape[0]
    value = value.astype(BF)
    act[1, pl.ds(row, rows), :] = value
    act[0, pl.ds(row, rows), :] = masked(pltpu.roll(value, 1, 1), lane_mask(1, LANES))
    act[2, pl.ds(row, rows), :] = masked(
        pltpu.roll(value, LANES - 1, 1), lane_mask(0, LANES - 1)
    )


def turned(value, lanes):
    return pltpu.roll(value, lanes % LANES, 1) if lanes % LANES else value


def pad_taps(weight, padded):
    taps, rows, cols = weight.shape
    for t in range(taps):
        padded[t, 0:rows, 0:cols] = weight[t]


def build_bands(padded, low, chans, wide, big, depth, da):
    parts = []
    for dz in range(3):
        taps = padded[9 * dz + 3 * da : 9 * dz + 3 * da + 3].reshape(3 * SLOT, LANES)
        if low or wide:
            taps = masked(taps, lane_mask(low, low + chans))
        parts.append(turned(taps, dz * SLOT - low))
    base = parts[0] + parts[1] + parts[2]
    for z in range(depth):
        moved = turned(base, (z - 1) * SLOT)
        if z == 0:
            moved = masked(moved, lane_mask(0, LANES - SLOT))
        if z == depth - 1:
            moved = masked(moved, lane_mask(SLOT, LANES))
        for dy in range(3):
            k = da * 3 + dy
            big[z * SLOT : (z + 1) * SLOT, k * LANES : (k + 1) * LANES] = moved[
                dy * SLOT : (dy + 1) * SLOT
            ]


def build_first(padded, big):
    parts = [padded[3 * da : 3 * da + 3].reshape(3 * SLOT, LANES) for da in range(3)]
    base = parts[0] + turned(parts[1], SLOT) + turned(parts[2], 2 * SLOT)
    for a in range(GROUP):
        moved = turned(base, a * SLOT)
        wide = masked(moved, lane_mask(a * SLOT, LANES))
        rest = masked(moved, lane_mask(0, (a - 1) * SLOT))
        rows = slice(a * SLOT, (a + 1) * SLOT)
        for dy in range(3):
            big[rows, dy * LANES : (dy + 1) * LANES] = wide[dy * SLOT : (dy + 1) * SLOT]
        half = [rest[dy * SLOT : (dy + 1) * SLOT] for dy in range(3)]
        big[rows, 3 * LANES : 4 * LANES] = half[0] + turned(half[1], LANES // 2)
        big[rows, 4 * LANES : 5 * LANES] = half[2]


def column(row_ref, pad, rows, pick):
    pad[...] = jnp.zeros(pad.shape, F32)
    pad[0:1, 0 : row_ref.shape[1]] = row_ref[...].astype(F32)
    spread = jnp.broadcast_to(pad[0:1, :], (rows, LANES))
    want = pick(lax.broadcasted_iota(jnp.int32, (rows, LANES), 0))
    return jnp.sum(jnp.where(lane_index(rows) == want, spread, 0.0), axis=1, keepdims=True)


def unet_kernel(
    owners,
    depth,
    first_block_h,
    offset_h,
    firsts_h,
    features,
    deep,
    w1,
    w2,
    w3,
    w4,
    b1_h,
    b2_h,
    b3_h,
    b4_h,
    hw_h,
    hb_h,
    wy_h,
    out,
    adder,
    first_block,
    offset,
    firsts_v,
    feat_v,
    deep_v,
    w1_v,
    w2_v,
    w3_v,
    w4_v,
    b1,
    b2,
    b3,
    b4,
    hw,
    hb,
    wy,
    cells,
    xf,
    x1,
    x2,
    xd,
    x3,
    m1,
    m2,
    m3s,
    m3d,
    m4t,
    m4f,
    p1,
    p2,
    p3,
    p4,
    pad,
    head,
    canvas,
    sems,
):
    chans, along, depth = feat_v.shape[0], feat_v.shape[1] // depth, depth
    plane = depth * SLOT
    me = lax.axis_index("segment")
    patch = lax.axis_index("patch") * features.shape[0] + me

    copies = [
        pltpu.make_async_copy(src, dst, sems.at[i])
        for i, (src, dst) in enumerate(
            [
                (features.at[me], feat_v),
                (w1, w1_v),
                (w2, w2_v),
                (deep.at[me], deep_v),
                (w3, w3_v),
                (w4, w4_v),
                (b1_h, b1),
                (b2_h, b2),
                (b3_h, b3),
                (b4_h, b4),
                (hw_h, hw),
                (hb_h, hb),
                (wy_h, wy),
                (first_block_h, first_block),
                (offset_h, offset),
                (firsts_h, firsts_v),
            ]
        )
    ]
    for c in copies:
        c.start()

    for act in (x1, x2, xd, x3):
        for dy in range(3):
            act[dy, 0:plane, :] = jnp.zeros((plane, LANES), BF)
            act[dy, (along + 1) * plane : (along + 2) * plane, :] = jnp.zeros((plane, LANES), BF)
    high = (along + 2) * SLOT
    for dy in range(3):
        for z in range(depth):
            xf[dy, z * high : z * high + SLOT, :] = jnp.zeros((SLOT, LANES), BF)
            xf[dy, (z + 1) * high - SLOT : (z + 1) * high, :] = jnp.zeros((SLOT, LANES), BF)
    for padded in (p1, p2, p3, p4):
        padded[...] = jnp.zeros(padded.shape, BF)
    head[...] = jnp.zeros(head.shape, F32)
    canvas[...] = jnp.zeros(canvas.shape, F32)
    used = chans * along * depth
    cells[used:, :] = jnp.zeros((cells.shape[0] - used, LANES), F32)

    def spread_cells(source):
        for c in range(chans):
            cells[pl.ds(c * along * depth, along * depth), :] = source[c].astype(F32)

    def gathered(z, a):
        return cells[pl.ds(a * depth + z, SLOT, stride=along * depth), :]

    def own(r):
        return r

    def make_adder(block, firsts):
        patches = firsts.shape[0]
        each = LANES // ROWS
        src = block * each + lane_index(patches) // ROWS
        sender = (src % owners) * features.shape[0] + src // owners
        mine = lax.broadcasted_iota(jnp.int32, (patches, LANES), 0) == sender
        first = jnp.sum(jnp.where(mine, firsts, 0.0), axis=0, keepdims=True).astype(jnp.int32)
        row = lax.broadcasted_iota(jnp.int32, (adder.shape[0], LANES), 0)
        lane = lane_index(adder.shape[0])
        ahead = (row // ROWS) * owners + lax.axis_index("patch") - first
        keep = (ahead >= 0) & (ahead < KMAX) & (row % ROWS == lane % ROWS)
        adder[:, block * LANES : (block + 1) * LANES] = jnp.where(keep, 1.0, 0.0).astype(BF)

    copies[0].wait()
    spread_cells(feat_v)
    for z in range(depth):
        for a in range(along):
            put_shifted(xf, z * high + (a + 1) * SLOT, gathered(z, a))

    copies[1].wait()
    pad_taps(w1_v, p1)
    build_first(p1, m1)
    for c in copies[2:]:
        c.wait()
    pad_taps(w2_v, p2)

    def bias_rows(ref, copies_of):
        col = column(ref, pad, SLOT, own)
        tile = jnp.broadcast_to(col, (SLOT, LANES))
        return jnp.concatenate([tile] * copies_of, axis=0)

    def matrix_tasks(padded, low, wide, big):
        return [
            functools.partial(build_bands, padded, low, chans, wide, big, depth, da)
            for da in range(3)
        ]

    def run(tasks, step, steps):
        for task in tasks[len(tasks) * step // steps : len(tasks) * (step + 1) // steps]:
            task()

    bias = bias_rows(b1, GROUP)
    bias2, bias3, bias4 = (bias_rows(b, depth) for b in (b2, b3, b4))
    tasks = matrix_tasks(p2, 0, False, m2)
    columns = [(z, group) for group in range(along // GROUP) for z in range(depth)]

    def first_window(z, group):
        low = z * high + group * GROUP * SLOT
        pieces = [xf[dy, pl.ds(low, LANES), :] for dy in range(3)]
        pieces += [xf[dy, pl.ds(low + LANES, LANES // 2), :] for dy in range(3)]
        return jnp.concatenate(pieces, axis=0)

    for pair in range(0, len(columns), 2):
        rhs = jnp.concatenate([first_window(*c) for c in columns[pair : pair + 2]], axis=1)
        got = jnp.dot(m1[:, 0 : rhs.shape[0]], rhs, preferred_element_type=F32)
        run(tasks, pair // 2, len(columns) // 2)
        for h, (z, group) in enumerate(columns[pair : pair + 2]):
            part = jnp.maximum(got[:, h * LANES : (h + 1) * LANES] + bias, 0.0)
            for a in range(GROUP):
                put_shifted(
                    x1,
                    (1 + group * GROUP + a) * plane + z * SLOT,
                    part[a * SLOT : (a + 1) * SLOT],
                )

    def window_of(act, a):
        return jnp.concatenate(
            [act[dy, pl.ds((a + da) * plane, plane), :] for da in range(3) for dy in range(3)],
            axis=0,
        )

    def conv(mats, acts, bias, a):
        matrix = jnp.concatenate([m[...] for m in mats], axis=1) if len(mats) > 1 else mats[0][...]
        cols = []
        for b in (a, a + 1):
            parts = [window_of(x, b) for x in acts]
            cols.append(jnp.concatenate(parts, axis=0) if len(parts) > 1 else parts[0])
        got = jnp.dot(matrix, jnp.concatenate(cols, axis=1), preferred_element_type=F32)
        wide = jnp.concatenate([bias, bias], axis=1)
        return jnp.maximum(got + wide, 0.0)

    def layer(mats, acts, bias, result, tasks):
        for a in range(0, along, 2):
            got = conv(mats, acts, bias, a)
            run(tasks, a // 2, along // 2)
            for h in range(2):
                put_shifted(result, (1 + a + h) * plane, got[:, h * LANES : (h + 1) * LANES])

    def deep_rows(a):
        for z in range(depth):
            put_shifted(xd, (a + 1) * plane + z * SLOT, gathered(z, a))

    pad_taps(w3_v, p3)
    spread_cells(deep_v)
    tasks = matrix_tasks(p3, 0, True, m3s) + matrix_tasks(p3, chans, True, m3d)
    tasks += [functools.partial(deep_rows, a) for a in range(along)]
    layer([m2], [x1], bias2, x2, tasks)
    pad_taps(w4_v, p4)
    tasks = matrix_tasks(p4, 0, True, m4t) + matrix_tasks(p4, chans, True, m4f)
    layer([m3s, m3d], [x2, xd], bias3, x3, tasks)
    bias = bias4
    kinds = hw.shape[0]
    tap = hw[...].astype(F32)
    for z in range(depth):
        head[z * 4 : z * 4 + kinds, z * SLOT : z * SLOT + chans] = tap
    head_b = head[...].astype(BF)
    head_bias = column(hb, pad, 4 * depth, lambda r: r % 4)
    sz, sa = bump(depth), bump(along)
    row = lax.broadcasted_iota(jnp.int32, (4 * depth, LANES), 0)
    blend_z = jnp.full((4 * depth, LANES), float(sz[0]), F32)
    for z in range(1, depth):
        blend_z = jnp.where(row >= 4 * z, float(sz[z]), blend_z)
    across = jnp.broadcast_to(wy[...], (4 * depth, LANES))
    start = first_block[patch]
    move = offset[patch]
    base = lax.rem(start, owners)
    firsts = column(firsts_v, pad, firsts_v.shape[1], own)
    tasks = [functools.partial(make_adder, b, firsts) for b in range(adder.shape[1] // LANES)]
    for a in range(0, along, 2):
        fourth = conv([m4t, m4f], [x3, x1], bias, a).astype(BF)
        logits = jnp.dot(head_b, fourth, preferred_element_type=F32) + head_bias
        run(tasks, a // 2, along // 2)
        value = jax.nn.sigmoid(logits)
        for h in range(2):
            part = value[:, h * LANES : (h + 1) * LANES] * (
                blend_z * float(sa[a + h]) * across
            )
            place = move + (a + h)
            owner = base + lax.div(place, CW)
            owner = jnp.where(owner >= owners, owner - owners, owner)
            spot = owner * ROWS + lax.rem(place, CW)
            for z in range(depth):
                for kind in range(kinds):
                    r = z * 4 + kind
                    canvas[pl.ds(spot + (z * owners * ROWS + kind * CW), 1), :] = part[r : r + 1, :]
    for slot in range(out.shape[0]):
        out[slot] = canvas[slot * ROWS : (slot + 1) * ROWS, :].astype(BF)


def blend_kernel(adder, mine, out):
    rows = mine[...].reshape(mine.shape[0] * ROWS, LANES)
    total = jnp.dot(adder[...], rows, preferred_element_type=F32)
    for i in range(out.shape[0]):
        for kind in range(out.shape[1]):
            lo = i * ROWS + kind * CW
            out[i, kind] = total[lo : lo + CW, :]


def held_in(space, *arrays):
    return [pltpu.with_memory_space_constraint(a, space) for a in arrays]


def per_device(
    features,
    deep_path,
    weight_first,
    bias_first,
    weight_second,
    bias_second,
    weight_third,
    bias_third,
    weight_fourth,
    bias_fourth,
    head_weight,
    head_bias,
    block_first,
    block_offset,
):
    segments = lax.axis_size("segment")
    owners = lax.axis_size("patch")
    count, chans, depth, along, across = features.shape
    kinds = head_weight.shape[0]
    assert count == segments and depth == segments and across == LANES
    assert block_first.shape[0] <= LANES and owners >= KMAX
    assert along % GROUP == 0 and kinds * CW <= ROWS and chans <= SLOT and depth * SLOT == LANES
    plane = depth * SLOT

    def by_cell(values):
        rows = (count, chans, along * depth, across)
        return values.transpose(0, 1, 3, 2, 4).reshape(rows)

    vmem = pl.BlockSpec(memory_space=pltpu.VMEM)
    hbm = pl.BlockSpec(memory_space=pltpu.HBM)
    act = pltpu.VMEM((3, (along + 2) * plane, LANES), BF)
    taps = pltpu.VMEM((plane, 9 * LANES), BF)
    wy = jnp.asarray(bump(across)).reshape(1, across)
    slots, adder = pl.pallas_call(
        functools.partial(unet_kernel, owners, depth),
        out_shape=(
            jax.ShapeDtypeStruct((segments * owners, ROWS, across), BF),
            jax.ShapeDtypeStruct((CH_DEV * ROWS, segments * owners * ROWS), BF),
        ),
        in_specs=[hbm] * 16,
        out_specs=(vmem, vmem),
        scratch_shapes=[
            pltpu.SMEM(block_first.shape, jnp.int32),
            pltpu.SMEM(block_first.shape, jnp.int32),
            pltpu.VMEM((1, block_first.shape[0]), jnp.int32),
            pltpu.VMEM((chans, along * depth, across), BF),
            pltpu.VMEM((chans, along * depth, across), BF),
            pltpu.VMEM(weight_first.shape, BF),
            pltpu.VMEM(weight_second.shape, BF),
            pltpu.VMEM(weight_third.shape, BF),
            pltpu.VMEM(weight_fourth.shape, BF),
            pltpu.VMEM((1, chans), F32),
            pltpu.VMEM((1, chans), F32),
            pltpu.VMEM((1, chans), F32),
            pltpu.VMEM((1, chans), F32),
            pltpu.VMEM(head_weight.shape, BF),
            pltpu.VMEM((1, kinds), F32),
            pltpu.VMEM((1, across), F32),
            pltpu.VMEM((SLOT * along * depth, LANES), F32),
            pltpu.VMEM((3, depth * (along + 2) * SLOT, LANES), BF),
            act,
            act,
            act,
            act,
            pltpu.VMEM((GROUP * SLOT, 5 * LANES), BF),
            taps,
            taps,
            taps,
            taps,
            taps,
            pltpu.VMEM((9, SLOT, LANES), BF),
            pltpu.VMEM((27, SLOT, LANES), BF),
            pltpu.VMEM((27, SLOT, LANES), BF),
            pltpu.VMEM((27, SLOT, LANES), BF),
            pltpu.VMEM((8, LANES), F32),
            pltpu.VMEM((4 * depth, LANES), F32),
            pltpu.VMEM((segments * owners * ROWS, LANES), F32),
            pltpu.SemaphoreType.DMA((16,)),
        ],
        compiler_params=pltpu.CompilerParams(vmem_limit_bytes=48 * 2**20),
    )(
        *held_in(
            pltpu.HBM,
        block_first,
        block_offset,
        block_first.reshape(1, -1),
        by_cell(features),
        by_cell(deep_path),
        weight_first,
        weight_second,
        weight_third,
        weight_fourth,
        bias_first.reshape(1, chans),
        bias_second.reshape(1, chans),
        bias_third.reshape(1, chans),
        bias_fourth.reshape(1, chans),
        head_weight,
        head_bias.reshape(1, kinds),
        wy,
        )
    )
    mine = lax.all_to_all(slots, ("segment", "patch"), split_axis=0, concat_axis=0, tiled=True)
    blended = pl.pallas_call(
        blend_kernel,
        out_shape=jax.ShapeDtypeStruct((CH_DEV, kinds, CW, across), F32),
        in_specs=[vmem, vmem],
        out_specs=vmem,
    )(*held_in(pltpu.VMEM, adder, mine))
    return blended.reshape(CH_DEV, 1, kinds, 1, CW, across)


def solution(mesh):
    rows = P("patch", None, None, None, None)
    return jax.shard_map(
        per_device,
        mesh=mesh,
        in_specs=(rows, rows) + (P(),) * 12,
        out_specs=P(None, "patch", None, "segment", None, None),
        check_vma=False,
    )
```

```python
import functools
import math

import jax
import jax.numpy as jnp
import numpy as np
from jax import lax
from jax.experimental import pallas as pl
from jax.experimental.pallas import tpu as pltpu
from jax.sharding import PartitionSpec as P

CW = 4
CH_DEV = 8
KMAX = 4
LANES = 128
SLOT = 32
TILE = 16
ROWS = 16
GROUP = 4
BF = jnp.bfloat16
F32 = jnp.float32


def bump(count):
    place = (np.arange(count).astype(np.float32) + np.float32(0.5)) / np.float32(count)
    return (np.sin(np.float32(np.pi) * place) ** 2).astype(np.float32)


def lane_index(rows):
    return lax.broadcasted_iota(jnp.int32, (rows, LANES), 1)


def lane_mask(low, high):
    lane = lane_index(TILE)
    return jnp.where((lane >= low) & (lane < high), 1.0, 0.0).astype(BF)


def masked(value, tile):
    rows = value.shape[0]
    return (value.reshape(rows // TILE, TILE, LANES) * tile[None]).reshape(rows, LANES)


def put_shifted(act, row, value):
    rows = value.shape[0]
    value = value.astype(BF)
    act[1, pl.ds(row, rows), :] = value
    act[0, pl.ds(row, rows), :] = masked(pltpu.roll(value, 1, 1), lane_mask(1, LANES))
    act[2, pl.ds(row, rows), :] = masked(
        pltpu.roll(value, LANES - 1, 1), lane_mask(0, LANES - 1)
    )


def turned(value, lanes):
    return pltpu.roll(value, lanes % LANES, 1) if lanes % LANES else value


def pad_taps(weight, padded):
    taps, rows, cols = weight.shape
    for t in range(taps):
        padded[t, 0:rows, 0:cols] = weight[t]


def build_bands(padded, low, chans, wide, big, depth, da):
    parts = []
    for dz in range(3):
        taps = padded[9 * dz + 3 * da : 9 * dz + 3 * da + 3].reshape(3 * SLOT, LANES)
        if low or wide:
            taps = masked(taps, lane_mask(low, low + chans))
        parts.append(turned(taps, dz * SLOT - low))
    base = parts[0] + parts[1] + parts[2]
    for z in range(depth):
        moved = turned(base, (z - 1) * SLOT)
        if z == 0:
            moved = masked(moved, lane_mask(0, LANES - SLOT))
        if z == depth - 1:
            moved = masked(moved, lane_mask(SLOT, LANES))
        for dy in range(3):
            k = da * 3 + dy
            big[z * SLOT : (z + 1) * SLOT, k * LANES : (k + 1) * LANES] = moved[
                dy * SLOT : (dy + 1) * SLOT
            ]


def build_first(padded, big):
    parts = [padded[3 * da : 3 * da + 3].reshape(3 * SLOT, LANES) for da in range(3)]
    base = parts[0] + turned(parts[1], SLOT) + turned(parts[2], 2 * SLOT)
    for a in range(GROUP):
        moved = turned(base, a * SLOT)
        wide = masked(moved, lane_mask(a * SLOT, LANES))
        rest = masked(moved, lane_mask(0, (a - 1) * SLOT))
        rows = slice(a * SLOT, (a + 1) * SLOT)
        for dy in range(3):
            big[rows, dy * LANES : (dy + 1) * LANES] = wide[dy * SLOT : (dy + 1) * SLOT]
        half = [rest[dy * SLOT : (dy + 1) * SLOT] for dy in range(3)]
        big[rows, 3 * LANES : 4 * LANES] = half[0] + turned(half[1], LANES // 2)
        big[rows, 4 * LANES : 5 * LANES] = half[2]


def column(row_ref, pad, rows, pick):
    pad[...] = jnp.zeros(pad.shape, F32)
    pad[0:1, 0 : row_ref.shape[1]] = row_ref[...].astype(F32)
    spread = jnp.broadcast_to(pad[0:1, :], (rows, LANES))
    want = pick(lax.broadcasted_iota(jnp.int32, (rows, LANES), 0))
    return jnp.sum(jnp.where(lane_index(rows) == want, spread, 0.0), axis=1, keepdims=True)


def unet_kernel(
    owners,
    depth,
    first_block_h,
    offset_h,
    firsts_h,
    features,
    deep,
    w1,
    w2,
    w3,
    w4,
    b1_h,
    b2_h,
    b3_h,
    b4_h,
    hw_h,
    hb_h,
    wy_h,
    out,
    adder,
    first_block,
    offset,
    firsts_v,
    feat_v,
    deep_v,
    w1_v,
    w2_v,
    w3_v,
    w4_v,
    b1,
    b2,
    b3,
    b4,
    hw,
    hb,
    wy,
    cells,
    xf,
    x1,
    x2,
    xd,
    x3,
    m1,
    m2,
    m3s,
    m3d,
    m4t,
    m4f,
    p1,
    p2,
    p3,
    p4,
    pad,
    head,
    canvas,
    sems,
):
    chans, along, depth = feat_v.shape[0], feat_v.shape[1] // depth, depth
    plane = depth * SLOT
    me = lax.axis_index("segment")
    patch = lax.axis_index("patch") * features.shape[0] + me

    copies = [
        pltpu.make_async_copy(src, dst, sems.at[i])
        for i, (src, dst) in enumerate(
            [
                (w1, w1_v),
                (features.at[me], feat_v),
                (w2, w2_v),
                (b1_h, b1),
                (w3, w3_v),
                (deep.at[me], deep_v),
                (w4, w4_v),
                (b2_h, b2),
                (b3_h, b3),
                (b4_h, b4),
                (hw_h, hw),
                (hb_h, hb),
                (wy_h, wy),
                (first_block_h, first_block),
                (offset_h, offset),
                (firsts_h, firsts_v),
            ]
        )
    ]
    for c in copies:
        c.start()

    for act in (x1, x2, xd, x3):
        for dy in range(3):
            act[dy, 0:plane, :] = jnp.zeros((plane, LANES), BF)
            act[dy, (along + 1) * plane : (along + 2) * plane, :] = jnp.zeros((plane, LANES), BF)
    high = (along + 2) * SLOT
    for dy in range(3):
        for z in range(depth):
            xf[dy, z * high : z * high + SLOT, :] = jnp.zeros((SLOT, LANES), BF)
            xf[dy, (z + 1) * high - SLOT : (z + 1) * high, :] = jnp.zeros((SLOT, LANES), BF)
    for padded in (p1, p2, p3, p4):
        padded[...] = jnp.zeros(padded.shape, BF)
    head[...] = jnp.zeros(head.shape, F32)
    canvas[...] = jnp.zeros(canvas.shape, F32)
    pitch = cells.shape[0] // SLOT
    used = chans * pitch
    cells[used:, :] = jnp.zeros((cells.shape[0] - used, LANES), F32)

    def spread_cells(source):
        for c in range(chans):
            cells[pl.ds(c * pitch, along * depth), :] = source[c].astype(F32)

    def gathered(z, a):
        return cells[pl.ds(a * depth + z, SLOT, stride=pitch), :]

    def own(r):
        return r

    def make_adder(block, firsts):
        patches = firsts.shape[0]
        each = LANES // ROWS
        src = block * each + lane_index(patches) // ROWS
        sender = (src % owners) * features.shape[0] + src // owners
        mine = lax.broadcasted_iota(jnp.int32, (patches, LANES), 0) == sender
        first = jnp.sum(jnp.where(mine, firsts, 0.0), axis=0, keepdims=True).astype(jnp.int32)
        row = lax.broadcasted_iota(jnp.int32, (adder.shape[0], LANES), 0)
        lane = lane_index(adder.shape[0])
        ahead = (row // ROWS) * owners + lax.axis_index("patch") - first
        keep = (ahead >= 0) & (ahead < KMAX) & (row % ROWS == lane % ROWS)
        adder[:, block * LANES : (block + 1) * LANES] = jnp.where(keep, 1.0, 0.0).astype(BF)

    def matrix_tasks(padded, low, wide, big):
        return [
            functools.partial(build_bands, padded, low, chans, wide, big, depth, da)
            for da in range(3)
        ]

    for c in copies[0:2]:
        c.wait()
    pad_taps(w1_v, p1)
    build_first(p1, m1)
    spread_cells(feat_v)
    for z in range(depth):
        for a in range(along):
            put_shifted(xf, z * high + (a + 1) * SLOT, gathered(z, a))

    for c in copies[2:]:
        c.wait()
    def bias_rows(ref, copies_of):
        col = column(ref, pad, SLOT, own)
        tile = jnp.broadcast_to(col, (SLOT, LANES))
        return jnp.concatenate([tile] * copies_of, axis=0)

    def run(tasks, step, steps):
        for task in tasks[len(tasks) * step // steps : len(tasks) * (step + 1) // steps]:
            task()

    bias = bias_rows(b1, GROUP)
    bias2, bias3, bias4 = (bias_rows(b, depth) for b in (b2, b3, b4))
    tasks = [functools.partial(pad_taps, w2_v, p2)] + matrix_tasks(p2, 0, False, m2) + [functools.partial(pad_taps, w3_v, p3)]
    columns = [(z, group) for group in range(along // GROUP) for z in range(depth)]

    def first_window(z, group):
        low = z * high + group * GROUP * SLOT
        pieces = [xf[dy, pl.ds(low, LANES), :] for dy in range(3)]
        pieces += [xf[dy, pl.ds(low + LANES, LANES // 2), :] for dy in range(3)]
        return jnp.concatenate(pieces, axis=0)

    for pair in range(0, len(columns), 2):
        rhs = jnp.concatenate([first_window(*c) for c in columns[pair : pair + 2]], axis=1)
        got = jnp.dot(m1[:, 0 : rhs.shape[0]], rhs, preferred_element_type=F32)
        run(tasks, pair // 2, len(columns) // 2)
        for h, (z, group) in enumerate(columns[pair : pair + 2]):
            part = jnp.maximum(got[:, h * LANES : (h + 1) * LANES] + bias, 0.0)
            for a in range(GROUP):
                put_shifted(
                    x1,
                    (1 + group * GROUP + a) * plane + z * SLOT,
                    part[a * SLOT : (a + 1) * SLOT],
                )

    def window_of(act, a):
        return jnp.concatenate(
            [act[dy, pl.ds((a + da) * plane, plane), :] for da in range(3) for dy in range(3)],
            axis=0,
        )

    def conv(mats, acts, bias, a):
        matrix = jnp.concatenate([m[...] for m in mats], axis=1) if len(mats) > 1 else mats[0][...]
        cols = []
        for b in (a, a + 1):
            parts = [window_of(x, b) for x in acts]
            cols.append(jnp.concatenate(parts, axis=0) if len(parts) > 1 else parts[0])
        got = jnp.dot(matrix, jnp.concatenate(cols, axis=1), preferred_element_type=F32)
        wide = jnp.concatenate([bias, bias], axis=1)
        return jnp.maximum(got + wide, 0.0)

    def layer(mats, acts, bias, result, tasks):
        for a in range(0, along, 2):
            got = conv(mats, acts, bias, a)
            run(tasks, a // 2, along // 2)
            for h in range(2):
                put_shifted(result, (1 + a + h) * plane, got[:, h * LANES : (h + 1) * LANES])

    def deep_rows(a):
        for z in range(depth):
            put_shifted(xd, (a + 1) * plane + z * SLOT, gathered(z, a))

    tasks = matrix_tasks(p3, 0, True, m3s) + matrix_tasks(p3, chans, True, m3d) + [functools.partial(spread_cells, deep_v)] + [functools.partial(deep_rows, a) for a in range(along)]
    layer([m2], [x1], bias2, x2, tasks)
    pad_taps(w4_v, p4)
    tasks = matrix_tasks(p4, 0, True, m4t) + matrix_tasks(p4, chans, True, m4f)
    layer([m3s, m3d], [x2, xd], bias3, x3, tasks)
    bias = bias4
    kinds = hw.shape[0]
    tap = hw[...].astype(F32)
    for z in range(depth):
        head[z * 4 : z * 4 + kinds, z * SLOT : z * SLOT + chans] = tap
    head_b = head[...].astype(BF)
    head_bias = column(hb, pad, 4 * depth, lambda r: r % 4)
    sz, sa = bump(depth), bump(along)
    row = lax.broadcasted_iota(jnp.int32, (4 * depth, LANES), 0)
    blend_z = jnp.full((4 * depth, LANES), float(sz[0]), F32)
    for z in range(1, depth):
        blend_z = jnp.where(row >= 4 * z, float(sz[z]), blend_z)
    across = jnp.broadcast_to(wy[...], (4 * depth, LANES))
    start = first_block[patch]
    move = offset[patch]
    base = lax.rem(start, owners)
    firsts = column(firsts_v, pad, firsts_v.shape[1], own)
    tasks = [functools.partial(make_adder, b, firsts) for b in range(adder.shape[1] // LANES)]
    for a in range(0, along, 2):
        fourth = conv([m4t, m4f], [x3, x1], bias, a).astype(BF)
        logits = jnp.dot(head_b, fourth, preferred_element_type=F32) + head_bias
        run(tasks, a // 2, along // 2)
        value = jax.nn.sigmoid(logits)
        for h in range(2):
            part = value[:, h * LANES : (h + 1) * LANES] * (
                blend_z * float(sa[a + h]) * across
            )
            place = move + (a + h)
            owner = base + lax.div(place, CW)
            owner = jnp.where(owner >= owners, owner - owners, owner)
            spot = owner * ROWS + lax.rem(place, CW)
            for z in range(depth):
                for kind in range(kinds):
                    r = z * 4 + kind
                    canvas[pl.ds(spot + (z * owners * ROWS + kind * CW), 1), :] = part[r : r + 1, :]
    for slot in range(out.shape[0]):
        out[slot] = canvas[slot * ROWS : (slot + 1) * ROWS, :].astype(BF)


def blend_kernel(adder, mine, out):
    rows = mine[...].reshape(mine.shape[0] * ROWS, LANES)
    total = jnp.dot(adder[...], rows, preferred_element_type=F32)
    for i in range(out.shape[0]):
        for kind in range(out.shape[1]):
            lo = i * ROWS + kind * CW
            out[i, kind] = total[lo : lo + CW, :]


def held_in(space, *arrays):
    return [pltpu.with_memory_space_constraint(a, space) for a in arrays]


def per_device(
    features,
    deep_path,
    weight_first,
    bias_first,
    weight_second,
    bias_second,
    weight_third,
    bias_third,
    weight_fourth,
    bias_fourth,
    head_weight,
    head_bias,
    block_first,
    block_offset,
):
    segments = lax.axis_size("segment")
    owners = lax.axis_size("patch")
    count, chans, depth, along, across = features.shape
    kinds = head_weight.shape[0]
    assert count == segments and depth == segments and across == LANES
    assert block_first.shape[0] <= LANES and owners >= KMAX
    assert along % GROUP == 0 and kinds * CW <= ROWS and chans <= SLOT and depth * SLOT == LANES
    plane = depth * SLOT

    def by_cell(values):
        rows = (count, chans, along * depth, across)
        return values.transpose(0, 1, 3, 2, 4).reshape(rows)

    vmem = pl.BlockSpec(memory_space=pltpu.VMEM)
    hbm = pl.BlockSpec(memory_space=pltpu.HBM)
    act = pltpu.VMEM((3, (along + 2) * plane, LANES), BF)
    taps = pltpu.VMEM((plane, 9 * LANES), BF)
    wy = jnp.asarray(bump(across)).reshape(1, across)
    slots, adder = pl.pallas_call(
        functools.partial(unet_kernel, owners, depth),
        out_shape=(
            jax.ShapeDtypeStruct((segments * owners, ROWS, across), BF),
            jax.ShapeDtypeStruct((CH_DEV * ROWS, segments * owners * ROWS), BF),
        ),
        in_specs=[hbm] * 16,
        out_specs=(vmem, vmem),
        scratch_shapes=[
            pltpu.SMEM(block_first.shape, jnp.int32),
            pltpu.SMEM(block_first.shape, jnp.int32),
            pltpu.VMEM((1, block_first.shape[0]), jnp.int32),
            pltpu.VMEM((chans, along * depth, across), BF),
            pltpu.VMEM((chans, along * depth, across), BF),
            pltpu.VMEM(weight_first.shape, BF),
            pltpu.VMEM(weight_second.shape, BF),
            pltpu.VMEM(weight_third.shape, BF),
            pltpu.VMEM(weight_fourth.shape, BF),
            pltpu.VMEM((1, chans), F32),
            pltpu.VMEM((1, chans), F32),
            pltpu.VMEM((1, chans), F32),
            pltpu.VMEM((1, chans), F32),
            pltpu.VMEM(head_weight.shape, BF),
            pltpu.VMEM((1, kinds), F32),
            pltpu.VMEM((1, across), F32),
            pltpu.VMEM((SLOT * (along * depth + 1), LANES), F32),
            pltpu.VMEM((3, depth * (along + 2) * SLOT, LANES), BF),
            act,
            act,
            act,
            act,
            pltpu.VMEM((GROUP * SLOT, 5 * LANES), BF),
            taps,
            taps,
            taps,
            taps,
            taps,
            pltpu.VMEM((9, SLOT, LANES), BF),
            pltpu.VMEM((27, SLOT, LANES), BF),
            pltpu.VMEM((27, SLOT, LANES), BF),
            pltpu.VMEM((27, SLOT, LANES), BF),
            pltpu.VMEM((8, LANES), F32),
            pltpu.VMEM((4 * depth, LANES), F32),
            pltpu.VMEM((segments * owners * ROWS, LANES), F32),
            pltpu.SemaphoreType.DMA((16,)),
        ],
        compiler_params=pltpu.CompilerParams(vmem_limit_bytes=48 * 2**20),
    )(
        *held_in(
            pltpu.HBM,
        block_first,
        block_offset,
        block_first.reshape(1, -1),
        by_cell(features),
        by_cell(deep_path),
        weight_first,
        weight_second,
        weight_third,
        weight_fourth,
        bias_first.reshape(1, chans),
        bias_second.reshape(1, chans),
        bias_third.reshape(1, chans),
        bias_fourth.reshape(1, chans),
        head_weight,
        head_bias.reshape(1, kinds),
        wy,
        )
    )
    mine = lax.all_to_all(slots, ("segment", "patch"), split_axis=0, concat_axis=0, tiled=True)
    blended = pl.pallas_call(
        blend_kernel,
        out_shape=jax.ShapeDtypeStruct((CH_DEV, kinds, CW, across), F32),
        in_specs=[vmem, vmem],
        out_specs=vmem,
    )(*held_in(pltpu.VMEM, adder, mine))
    return blended.reshape(CH_DEV, 1, kinds, 1, CW, across)


def solution(mesh):
    rows = P("patch", None, None, None, None)
    return jax.shard_map(
        per_device,
        mesh=mesh,
        in_specs=(rows, rows) + (P(),) * 12,
        out_specs=P(None, "patch", None, "segment", None, None),
        check_vma=False,
    )
```

```python
import functools
import math

import jax
import jax.numpy as jnp
import numpy as np
from jax import lax
from jax.experimental import pallas as pl
from jax.experimental.pallas import tpu as pltpu
from jax.sharding import PartitionSpec as P

CW = 4
CH_DEV = 8
KMAX = 4
LANES = 128
SLOT = 32
TILE = 16
ROWS = 16
GROUP = 4
BF = jnp.bfloat16
F32 = jnp.float32


def bump(count):
    place = (np.arange(count).astype(np.float32) + np.float32(0.5)) / np.float32(count)
    return (np.sin(np.float32(np.pi) * place) ** 2).astype(np.float32)


def lane_index(rows):
    return lax.broadcasted_iota(jnp.int32, (rows, LANES), 1)


def lane_mask(low, high):
    lane = lane_index(TILE)
    return jnp.where((lane >= low) & (lane < high), 1.0, 0.0).astype(BF)


def masked(value, tile):
    rows = value.shape[0]
    return (value.reshape(rows // TILE, TILE, LANES) * tile[None]).reshape(rows, LANES)


def put_shifted(act, row, value):
    rows = value.shape[0]
    value = value.astype(BF)
    act[1, pl.ds(row, rows), :] = value
    act[0, pl.ds(row, rows), :] = masked(pltpu.roll(value, 1, 1), lane_mask(1, LANES))
    act[2, pl.ds(row, rows), :] = masked(
        pltpu.roll(value, LANES - 1, 1), lane_mask(0, LANES - 1)
    )


def turned(value, lanes):
    return pltpu.roll(value, lanes % LANES, 1) if lanes % LANES else value


def pad_taps(weight, padded):
    taps, rows, cols = weight.shape
    for t in range(taps):
        padded[t, 0:rows, 0:cols] = weight[t]


def build_bases(padded, low, chans, wide, bases, place, da):
    parts = []
    for dz in range(3):
        taps = padded[9 * dz + 3 * da : 9 * dz + 3 * da + 3].reshape(3 * SLOT, LANES)
        if low or wide:
            taps = masked(taps, lane_mask(low, low + chans))
        parts.append(turned(taps, dz * chans - low))
    first = (place + 3 * da) * SLOT
    bases[first : first + 3 * SLOT, :] = parts[0] + parts[1] + parts[2]


def build_rows(bases, blocks, chans, big, depth, z):
    dense = depth * chans
    columns = {}
    for k in range(blocks):
        moved = turned(bases[k * SLOT : (k + 1) * SLOT, :], k * dense + (z - 1) * chans)
        low = k * dense + max(z - 1, 0) * chans
        high = k * dense + min(z + 2, depth) * chans
        for j in range(low // LANES, (high - 1) // LANES + 1):
            tile = lane_mask(max(low - j * LANES, 0), min(high - j * LANES, LANES))
            piece = masked(moved, tile)
            columns[j] = columns[j] + piece if j in columns else piece
    for j, value in columns.items():
        lanes = min(LANES, blocks * dense - j * LANES)
        big[z * chans : (z + 1) * chans, j * LANES : j * LANES + lanes] = value[:chans, :lanes]


def build_first(padded, big):
    parts = [padded[3 * da : 3 * da + 3].reshape(3 * SLOT, LANES) for da in range(3)]
    base = parts[0] + turned(parts[1], SLOT) + turned(parts[2], 2 * SLOT)
    for a in range(GROUP):
        moved = turned(base, a * SLOT)
        wide = masked(moved, lane_mask(a * SLOT, LANES))
        rest = masked(moved, lane_mask(0, (a - 1) * SLOT))
        rows = slice(a * SLOT, (a + 1) * SLOT)
        for dy in range(3):
            big[rows, dy * LANES : (dy + 1) * LANES] = wide[dy * SLOT : (dy + 1) * SLOT]
        half = [rest[dy * SLOT : (dy + 1) * SLOT] for dy in range(3)]
        big[rows, 3 * LANES : 4 * LANES] = half[0] + turned(half[1], LANES // 2)
        big[rows, 4 * LANES : 5 * LANES] = half[2]


def column(row_ref, pad, rows, pick):
    pad[...] = jnp.zeros(pad.shape, F32)
    pad[0:1, 0 : row_ref.shape[1]] = row_ref[...].astype(F32)
    spread = jnp.broadcast_to(pad[0:1, :], (rows, LANES))
    want = pick(lax.broadcasted_iota(jnp.int32, (rows, LANES), 0))
    return jnp.sum(jnp.where(lane_index(rows) == want, spread, 0.0), axis=1, keepdims=True)


def unet_kernel(
    owners,
    depth,
    first_block_h,
    offset_h,
    firsts_h,
    features,
    deep,
    w1,
    w2,
    w3,
    w4,
    b1_h,
    b2_h,
    b3_h,
    b4_h,
    hw_h,
    hb_h,
    wy_h,
    out,
    adder,
    first_block,
    offset,
    firsts_v,
    feat_v,
    deep_v,
    w1_v,
    w2_v,
    w3_v,
    w4_v,
    b1,
    b2,
    b3,
    b4,
    hw,
    hb,
    wy,
    cells,
    xf,
    x1,
    x2,
    xd,
    x3,
    m1,
    m2,
    m3,
    m4,
    q2,
    q3,
    q4,
    p1,
    p2,
    p3,
    p4,
    pad,
    head,
    canvas,
    sems,
):
    chans, along, depth = feat_v.shape[0], feat_v.shape[1] // depth, depth
    dense = depth * chans
    me = lax.axis_index("segment")
    patch = lax.axis_index("patch") * features.shape[0] + me

    copies = [
        pltpu.make_async_copy(src, dst, sems.at[i])
        for i, (src, dst) in enumerate(
            [
                (w1, w1_v),
                (features.at[me], feat_v),
                (w2, w2_v),
                (b1_h, b1),
                (w3, w3_v),
                (deep.at[me], deep_v),
                (w4, w4_v),
                (b2_h, b2),
                (b3_h, b3),
                (b4_h, b4),
                (hw_h, hw),
                (hb_h, hb),
                (wy_h, wy),
                (first_block_h, first_block),
                (offset_h, offset),
                (firsts_h, firsts_v),
            ]
        )
    ]
    for c in copies:
        c.start()

    for act in (x1, x2, xd, x3):
        for dy in range(3):
            act[dy, 0:dense, :] = jnp.zeros((dense, LANES), BF)
            act[dy, (along + 1) * dense : (along + 2) * dense, :] = jnp.zeros((dense, LANES), BF)
    high = (along + 2) * SLOT
    for dy in range(3):
        for z in range(depth):
            xf[dy, z * high : z * high + SLOT, :] = jnp.zeros((SLOT, LANES), BF)
            xf[dy, (z + 1) * high - SLOT : (z + 1) * high, :] = jnp.zeros((SLOT, LANES), BF)
    for padded in (p1, p2, p3, p4):
        padded[...] = jnp.zeros(padded.shape, BF)
    head[...] = jnp.zeros(head.shape, F32)
    canvas[...] = jnp.zeros(canvas.shape, F32)
    pitch = cells.shape[0] // SLOT
    used = chans * pitch
    cells[used:, :] = jnp.zeros((cells.shape[0] - used, LANES), F32)

    def spread_cells(source):
        for c in range(chans):
            cells[pl.ds(c * pitch, along * depth), :] = source[c].astype(F32)

    def gathered(z, a):
        return cells[pl.ds(a * depth + z, SLOT, stride=pitch), :]

    def own(r):
        return r

    def make_adder(block, firsts):
        patches = firsts.shape[0]
        each = LANES // ROWS
        src = block * each + lane_index(patches) // ROWS
        sender = (src % owners) * features.shape[0] + src // owners
        mine = lax.broadcasted_iota(jnp.int32, (patches, LANES), 0) == sender
        first = jnp.sum(jnp.where(mine, firsts, 0.0), axis=0, keepdims=True).astype(jnp.int32)
        row = lax.broadcasted_iota(jnp.int32, (adder.shape[0], LANES), 0)
        lane = lane_index(adder.shape[0])
        ahead = (row // ROWS) * owners + lax.axis_index("patch") - first
        keep = (ahead >= 0) & (ahead < KMAX) & (row % ROWS == lane % ROWS)
        adder[:, block * LANES : (block + 1) * LANES] = jnp.where(keep, 1.0, 0.0).astype(BF)

    def matrix_tasks(padded, bases, big):
        sources = big.shape[1] // (9 * dense)
        tasks = [
            functools.partial(
                build_bases, padded, i * chans, chans, sources > 1, bases, 9 * i, da
            )
            for i in range(sources)
            for da in range(3)
        ]
        return tasks + [
            functools.partial(build_rows, bases, 9 * sources, chans, big, depth, z)
            for z in range(depth)
        ]

    for c in copies[0:2]:
        c.wait()
    pad_taps(w1_v, p1)
    build_first(p1, m1)
    spread_cells(feat_v)
    for z in range(depth):
        for a in range(along):
            put_shifted(xf, z * high + (a + 1) * SLOT, gathered(z, a))

    for c in copies[2:]:
        c.wait()
    def bias_rows(ref, rows, each):
        return jnp.broadcast_to(column(ref, pad, rows, lambda r: r % each), (rows, LANES))

    def run(tasks, step, steps):
        for task in tasks[len(tasks) * step // steps : len(tasks) * (step + 1) // steps]:
            task()

    bias = bias_rows(b1, GROUP * SLOT, SLOT)
    bias2, bias3, bias4 = (bias_rows(b, dense, chans) for b in (b2, b3, b4))
    tasks = [functools.partial(pad_taps, w2_v, p2)] + matrix_tasks(p2, q2, m2) + [functools.partial(pad_taps, w3_v, p3)]
    columns = [(z, group) for group in range(along // GROUP) for z in range(depth)]

    def first_window(z, group):
        low = z * high + group * GROUP * SLOT
        pieces = [xf[dy, pl.ds(low, LANES), :] for dy in range(3)]
        pieces += [xf[dy, pl.ds(low + LANES, LANES // 2), :] for dy in range(3)]
        return jnp.concatenate(pieces, axis=0)

    sections = []
    for pair in range(0, len(columns), 2):
        rhs = jnp.concatenate([first_window(*c) for c in columns[pair : pair + 2]], axis=1)
        got = jnp.dot(m1[:, 0 : rhs.shape[0]], rhs, preferred_element_type=F32)
        run(tasks, pair // 2, len(columns) // 2)
        for h, (z, group) in enumerate(columns[pair : pair + 2]):
            sections.append(jnp.maximum(got[:, h * LANES : (h + 1) * LANES] + bias, 0.0))
            if len(sections) < depth:
                continue
            for a in range(GROUP):
                low = a * SLOT
                put_shifted(
                    x1,
                    (1 + group * GROUP + a) * dense,
                    jnp.concatenate([part[low : low + chans] for part in sections], axis=0),
                )
            sections = []

    def window_of(act, a):
        return jnp.concatenate(
            [act[dy, pl.ds((a + da) * dense, dense), :] for da in range(3) for dy in range(3)],
            axis=0,
        )

    def conv(matrix, acts, bias, a):
        cols = []
        for b in (a, a + 1):
            parts = [window_of(x, b) for x in acts]
            cols.append(jnp.concatenate(parts, axis=0) if len(parts) > 1 else parts[0])
        got = jnp.dot(matrix[...], jnp.concatenate(cols, axis=1), preferred_element_type=F32)
        wide = jnp.concatenate([bias, bias], axis=1)
        return jnp.maximum(got + wide, 0.0)

    def layer(matrix, acts, bias, result, tasks):
        for a in range(0, along, 2):
            got = conv(matrix, acts, bias, a)
            run(tasks, a // 2, along // 2)
            for h in range(2):
                put_shifted(result, (1 + a + h) * dense, got[:, h * LANES : (h + 1) * LANES])

    def deep_rows(a):
        value = jnp.concatenate([gathered(z, a)[:chans] for z in range(depth)], axis=0)
        put_shifted(xd, (a + 1) * dense, value)

    tasks = matrix_tasks(p3, q3, m3) + [functools.partial(spread_cells, deep_v)] + [functools.partial(deep_rows, a) for a in range(along)]
    layer(m2, [x1], bias2, x2, tasks)
    pad_taps(w4_v, p4)
    tasks = matrix_tasks(p4, q4, m4)
    layer(m3, [x2, xd], bias3, x3, tasks)
    bias = bias4
    kinds = hw.shape[0]
    tap = hw[...].astype(F32)
    for z in range(depth):
        head[z * 4 : z * 4 + kinds, z * chans : (z + 1) * chans] = tap
    head_b = head[:, 0:dense].astype(BF)
    head_bias = column(hb, pad, 4 * depth, lambda r: r % 4)
    sz, sa = bump(depth), bump(along)
    row = lax.broadcasted_iota(jnp.int32, (4 * depth, LANES), 0)
    blend_z = jnp.full((4 * depth, LANES), float(sz[0]), F32)
    for z in range(1, depth):
        blend_z = jnp.where(row >= 4 * z, float(sz[z]), blend_z)
    across = jnp.broadcast_to(wy[...], (4 * depth, LANES))
    start = first_block[patch]
    move = offset[patch]
    base = lax.rem(start, owners)
    firsts = column(firsts_v, pad, firsts_v.shape[1], own)
    tasks = [functools.partial(make_adder, b, firsts) for b in range(adder.shape[1] // LANES)]
    for a in range(0, along, 2):
        fourth = conv(m4, [x3, x1], bias, a).astype(BF)
        logits = jnp.dot(head_b, fourth, preferred_element_type=F32) + head_bias
        run(tasks, a // 2, along // 2)
        value = jax.nn.sigmoid(logits)
        for h in range(2):
            part = value[:, h * LANES : (h + 1) * LANES] * (
                blend_z * float(sa[a + h]) * across
            )
            place = move + (a + h)
            owner = base + lax.div(place, CW)
            owner = jnp.where(owner >= owners, owner - owners, owner)
            spot = owner * ROWS + lax.rem(place, CW)
            for z in range(depth):
                for kind in range(kinds):
                    r = z * 4 + kind
                    canvas[pl.ds(spot + (z * owners * ROWS + kind * CW), 1), :] = part[r : r + 1, :]
    for slot in range(out.shape[0]):
        out[slot] = canvas[slot * ROWS : (slot + 1) * ROWS, :].astype(BF)


def blend_kernel(adder, mine, out):
    rows = mine[...].reshape(mine.shape[0] * ROWS, LANES)
    total = jnp.dot(adder[...], rows, preferred_element_type=F32)
    for i in range(out.shape[0]):
        for kind in range(out.shape[1]):
            lo = i * ROWS + kind * CW
            out[i, kind] = total[lo : lo + CW, :]


def held_in(space, *arrays):
    return [pltpu.with_memory_space_constraint(a, space) for a in arrays]


def per_device(
    features,
    deep_path,
    weight_first,
    bias_first,
    weight_second,
    bias_second,
    weight_third,
    bias_third,
    weight_fourth,
    bias_fourth,
    head_weight,
    head_bias,
    block_first,
    block_offset,
):
    segments = lax.axis_size("segment")
    owners = lax.axis_size("patch")
    count, chans, depth, along, across = features.shape
    kinds = head_weight.shape[0]
    assert count == segments and depth == segments and across == LANES
    assert block_first.shape[0] <= LANES and owners >= KMAX
    assert along % GROUP == 0 and kinds * CW <= ROWS and chans <= SLOT and depth * SLOT == LANES
    dense = depth * chans
    assert dense % TILE == 0

    def by_cell(values):
        rows = (count, chans, along * depth, across)
        return values.transpose(0, 1, 3, 2, 4).reshape(rows)

    vmem = pl.BlockSpec(memory_space=pltpu.VMEM)
    hbm = pl.BlockSpec(memory_space=pltpu.HBM)
    act = pltpu.VMEM((3, (along + 2) * dense, LANES), BF)
    one = pltpu.VMEM((dense, 9 * dense), BF)
    two = pltpu.VMEM((dense, 18 * dense), BF)
    wy = jnp.asarray(bump(across)).reshape(1, across)
    slots, adder = pl.pallas_call(
        functools.partial(unet_kernel, owners, depth),
        out_shape=(
            jax.ShapeDtypeStruct((segments * owners, ROWS, across), BF),
            jax.ShapeDtypeStruct((CH_DEV * ROWS, segments * owners * ROWS), BF),
        ),
        in_specs=[hbm] * 16,
        out_specs=(vmem, vmem),
        scratch_shapes=[
            pltpu.SMEM(block_first.shape, jnp.int32),
            pltpu.SMEM(block_first.shape, jnp.int32),
            pltpu.VMEM((1, block_first.shape[0]), jnp.int32),
            pltpu.VMEM((chans, along * depth, across), BF),
            pltpu.VMEM((chans, along * depth, across), BF),
            pltpu.VMEM(weight_first.shape, BF),
            pltpu.VMEM(weight_second.shape, BF),
            pltpu.VMEM(weight_third.shape, BF),
            pltpu.VMEM(weight_fourth.shape, BF),
            pltpu.VMEM((1, chans), F32),
            pltpu.VMEM((1, chans), F32),
            pltpu.VMEM((1, chans), F32),
            pltpu.VMEM((1, chans), F32),
            pltpu.VMEM(head_weight.shape, BF),
            pltpu.VMEM((1, kinds), F32),
            pltpu.VMEM((1, across), F32),
            pltpu.VMEM((SLOT * (along * depth + 1), LANES), F32),
            pltpu.VMEM((3, depth * (along + 2) * SLOT, LANES), BF),
            act,
            act,
            act,
            act,
            pltpu.VMEM((GROUP * SLOT, 5 * LANES), BF),
            one,
            two,
            two,
            pltpu.VMEM((9 * SLOT, LANES), BF),
            pltpu.VMEM((18 * SLOT, LANES), BF),
            pltpu.VMEM((18 * SLOT, LANES), BF),
            pltpu.VMEM((9, SLOT, LANES), BF),
            pltpu.VMEM((27, SLOT, LANES), BF),
            pltpu.VMEM((27, SLOT, LANES), BF),
            pltpu.VMEM((27, SLOT, LANES), BF),
            pltpu.VMEM((8, LANES), F32),
            pltpu.VMEM((4 * depth, LANES), F32),
            pltpu.VMEM((segments * owners * ROWS, LANES), F32),
            pltpu.SemaphoreType.DMA((16,)),
        ],
        compiler_params=pltpu.CompilerParams(vmem_limit_bytes=48 * 2**20),
    )(
        *held_in(
            pltpu.HBM,
        block_first,
        block_offset,
        block_first.reshape(1, -1),
        by_cell(features),
        by_cell(deep_path),
        weight_first,
        weight_second,
        weight_third,
        weight_fourth,
        bias_first.reshape(1, chans),
        bias_second.reshape(1, chans),
        bias_third.reshape(1, chans),
        bias_fourth.reshape(1, chans),
        head_weight,
        head_bias.reshape(1, kinds),
        wy,
        )
    )
    mine = lax.all_to_all(slots, ("segment", "patch"), split_axis=0, concat_axis=0, tiled=True)
    blended = pl.pallas_call(
        blend_kernel,
        out_shape=jax.ShapeDtypeStruct((CH_DEV, kinds, CW, across), F32),
        in_specs=[vmem, vmem],
        out_specs=vmem,
    )(*held_in(pltpu.VMEM, adder, mine))
    return blended.reshape(CH_DEV, 1, kinds, 1, CW, across)


def solution(mesh):
    rows = P("patch", None, None, None, None)
    return jax.shard_map(
        per_device,
        mesh=mesh,
        in_specs=(rows, rows) + (P(),) * 12,
        out_specs=P(None, "patch", None, "segment", None, None),
        check_vma=False,
    )
```

```python
import functools
import math

import jax
import jax.numpy as jnp
import numpy as np
from jax import lax
from jax.experimental import pallas as pl
from jax.experimental.pallas import tpu as pltpu
from jax.sharding import PartitionSpec as P

CW = 4
CH_DEV = 8
KMAX = 4
LANES = 128
SLOT = 32
TILE = 16
ROWS = 16
WIDE = 4
GROUP = 4
BF = jnp.bfloat16
F32 = jnp.float32


def bump(count):
    place = (np.arange(count).astype(np.float32) + np.float32(0.5)) / np.float32(count)
    return (np.sin(np.float32(np.pi) * place) ** 2).astype(np.float32)


def lane_index(rows):
    return lax.broadcasted_iota(jnp.int32, (rows, LANES), 1)


def lane_mask(low, high):
    lane = lane_index(TILE)
    return jnp.where((lane >= low) & (lane < high), 1.0, 0.0).astype(BF)


def masked(value, tile):
    rows = value.shape[0]
    return (value.reshape(rows // TILE, TILE, LANES) * tile[None]).reshape(rows, LANES)


def put_shifted(act, row, value):
    rows = value.shape[0]
    value = value.astype(BF)
    act[1, pl.ds(row, rows), :] = value
    act[0, pl.ds(row, rows), :] = masked(pltpu.roll(value, 1, 1), lane_mask(1, LANES))
    act[2, pl.ds(row, rows), :] = masked(
        pltpu.roll(value, LANES - 1, 1), lane_mask(0, LANES - 1)
    )


def turned(value, lanes):
    return pltpu.roll(value, lanes % LANES, 1) if lanes % LANES else value


def pad_taps(weight, padded):
    taps, rows, cols = weight.shape
    for t in range(taps):
        padded[t, 0:rows, 0:cols] = weight[t]


def build_bases(padded, low, chans, wide, bases, place, da):
    parts = []
    for dz in range(3):
        taps = padded[9 * dz + 3 * da : 9 * dz + 3 * da + 3].reshape(3 * SLOT, LANES)
        if low or wide:
            taps = masked(taps, lane_mask(low, low + chans))
        parts.append(turned(taps, dz * chans - low))
    first = (place + 3 * da) * SLOT
    bases[first : first + 3 * SLOT, :] = parts[0] + parts[1] + parts[2]


def build_rows(bases, blocks, chans, big, depth, z):
    dense = depth * chans
    columns = {}
    for k in range(blocks):
        moved = turned(bases[k * SLOT : (k + 1) * SLOT, :], k * dense + (z - 1) * chans)
        low = k * dense + max(z - 1, 0) * chans
        high = k * dense + min(z + 2, depth) * chans
        for j in range(low // LANES, (high - 1) // LANES + 1):
            tile = lane_mask(max(low - j * LANES, 0), min(high - j * LANES, LANES))
            piece = masked(moved, tile)
            columns[j] = columns[j] + piece if j in columns else piece
    for j, value in columns.items():
        lanes = min(LANES, blocks * dense - j * LANES)
        big[z * chans : (z + 1) * chans, j * LANES : j * LANES + lanes] = value[:chans, :lanes]


def build_first(padded, big):
    parts = [padded[3 * da : 3 * da + 3].reshape(3 * SLOT, LANES) for da in range(3)]
    base = parts[0] + turned(parts[1], SLOT) + turned(parts[2], 2 * SLOT)
    for a in range(GROUP):
        moved = turned(base, a * SLOT)
        wide = masked(moved, lane_mask(a * SLOT, LANES))
        rest = masked(moved, lane_mask(0, (a - 1) * SLOT))
        rows = slice(a * SLOT, (a + 1) * SLOT)
        for dy in range(3):
            big[rows, dy * LANES : (dy + 1) * LANES] = wide[dy * SLOT : (dy + 1) * SLOT]
        half = [rest[dy * SLOT : (dy + 1) * SLOT] for dy in range(3)]
        big[rows, 3 * LANES : 4 * LANES] = half[0] + turned(half[1], LANES // 2)
        big[rows, 4 * LANES : 5 * LANES] = half[2]


def column(row_ref, pad, rows, pick):
    pad[...] = jnp.zeros(pad.shape, F32)
    pad[0:1, 0 : row_ref.shape[1]] = row_ref[...].astype(F32)
    spread = jnp.broadcast_to(pad[0:1, :], (rows, LANES))
    want = pick(lax.broadcasted_iota(jnp.int32, (rows, LANES), 0))
    return jnp.sum(jnp.where(lane_index(rows) == want, spread, 0.0), axis=1, keepdims=True)


def unet_kernel(
    owners,
    depth,
    first_block_h,
    offset_h,
    firsts_h,
    features,
    deep,
    w1,
    w2,
    w3,
    w4,
    b1_h,
    b2_h,
    b3_h,
    b4_h,
    hw_h,
    hb_h,
    wy_h,
    out,
    adder,
    first_block,
    offset,
    firsts_v,
    feat_v,
    deep_v,
    w1_v,
    w2_v,
    w3_v,
    w4_v,
    b1,
    b2,
    b3,
    b4,
    hw,
    hb,
    wy,
    cells,
    xf,
    x1,
    x2,
    xd,
    x3,
    m1,
    m2,
    m3,
    m4,
    q2,
    q3,
    q4,
    p1,
    p2,
    p3,
    p4,
    pad,
    head,
    canvas,
    sems,
):
    chans, along, depth = feat_v.shape[0], feat_v.shape[1] // depth, depth
    dense = depth * chans
    me = lax.axis_index("segment")
    patch = lax.axis_index("patch") * features.shape[0] + me

    copies = [
        pltpu.make_async_copy(src, dst, sems.at[i])
        for i, (src, dst) in enumerate(
            [
                (w1, w1_v),
                (features.at[me], feat_v),
                (w2, w2_v),
                (b1_h, b1),
                (w3, w3_v),
                (deep.at[me], deep_v),
                (w4, w4_v),
                (b2_h, b2),
                (b3_h, b3),
                (b4_h, b4),
                (hw_h, hw),
                (hb_h, hb),
                (wy_h, wy),
                (first_block_h, first_block),
                (offset_h, offset),
                (firsts_h, firsts_v),
            ]
        )
    ]
    for c in copies:
        c.start()

    for act in (x1, x2, xd, x3):
        for dy in range(3):
            act[dy, 0:dense, :] = jnp.zeros((dense, LANES), BF)
            act[dy, (along + 1) * dense : (along + 2) * dense, :] = jnp.zeros((dense, LANES), BF)
    high = (along + 2) * SLOT
    for dy in range(3):
        for z in range(depth):
            xf[dy, z * high : z * high + SLOT, :] = jnp.zeros((SLOT, LANES), BF)
            xf[dy, (z + 1) * high - SLOT : (z + 1) * high, :] = jnp.zeros((SLOT, LANES), BF)
    for padded in (p1, p2, p3, p4):
        padded[...] = jnp.zeros(padded.shape, BF)
    head[...] = jnp.zeros(head.shape, F32)
    canvas[...] = jnp.zeros(canvas.shape, F32)
    pitch = cells.shape[0] // SLOT
    used = chans * pitch
    cells[used:, :] = jnp.zeros((cells.shape[0] - used, LANES), F32)

    def spread_cells(source):
        for c in range(chans):
            cells[pl.ds(c * pitch, along * depth), :] = source[c].astype(F32)

    def gathered(z, a):
        return cells[pl.ds(a * depth + z, SLOT, stride=pitch), :]

    def own(r):
        return r

    def make_adder(block, firsts):
        patches = firsts.shape[0]
        each = LANES // ROWS
        src = block * each + lane_index(patches) // ROWS
        sender = (src % owners) * features.shape[0] + src // owners
        mine = lax.broadcasted_iota(jnp.int32, (patches, LANES), 0) == sender
        first = jnp.sum(jnp.where(mine, firsts, 0.0), axis=0, keepdims=True).astype(jnp.int32)
        row = lax.broadcasted_iota(jnp.int32, (adder.shape[0], LANES), 0)
        lane = lane_index(adder.shape[0])
        ahead = (row // ROWS) * owners + lax.axis_index("patch") - first
        keep = (ahead >= 0) & (ahead < KMAX) & (row % ROWS == lane % ROWS)
        adder[:, block * LANES : (block + 1) * LANES] = jnp.where(keep, 1.0, 0.0).astype(BF)

    def matrix_tasks(padded, bases, big):
        sources = big.shape[1] // (9 * dense)
        tasks = [
            functools.partial(
                build_bases, padded, i * chans, chans, sources > 1, bases, 9 * i, da
            )
            for i in range(sources)
            for da in range(3)
        ]
        return tasks + [
            functools.partial(build_rows, bases, 9 * sources, chans, big, depth, z)
            for z in range(depth)
        ]

    for c in copies[0:2]:
        c.wait()
    pad_taps(w1_v, p1)
    build_first(p1, m1)
    spread_cells(feat_v)
    for z in range(depth):
        for a in range(along):
            put_shifted(xf, z * high + (a + 1) * SLOT, gathered(z, a))

    for c in copies[2:]:
        c.wait()
    def bias_rows(ref, rows, each):
        return jnp.broadcast_to(column(ref, pad, rows, lambda r: r % each), (rows, LANES))

    def run(tasks, step, steps):
        for task in tasks[len(tasks) * step // steps : len(tasks) * (step + 1) // steps]:
            task()

    bias = bias_rows(b1, GROUP * SLOT, SLOT)
    bias2, bias3, bias4 = (bias_rows(b, dense, chans) for b in (b2, b3, b4))
    tasks = [functools.partial(pad_taps, w2_v, p2)] + matrix_tasks(p2, q2, m2) + [functools.partial(pad_taps, w3_v, p3)]
    columns = [(z, group) for group in range(along // GROUP) for z in range(depth)]

    def first_window(z, group):
        low = z * high + group * GROUP * SLOT
        pieces = [xf[dy, pl.ds(low, LANES), :] for dy in range(3)]
        pieces += [xf[dy, pl.ds(low + LANES, LANES // 2), :] for dy in range(3)]
        return jnp.concatenate(pieces, axis=0)

    sections = []
    for pair in range(0, len(columns), 2):
        rhs = jnp.concatenate([first_window(*c) for c in columns[pair : pair + 2]], axis=1)
        got = jnp.dot(m1[:, 0 : rhs.shape[0]], rhs, preferred_element_type=F32)
        run(tasks, pair // 2, len(columns) // 2)
        for h, (z, group) in enumerate(columns[pair : pair + 2]):
            sections.append(jnp.maximum(got[:, h * LANES : (h + 1) * LANES] + bias, 0.0))
            if len(sections) < depth:
                continue
            for a in range(GROUP):
                low = a * SLOT
                put_shifted(
                    x1,
                    (1 + group * GROUP + a) * dense,
                    jnp.concatenate([part[low : low + chans] for part in sections], axis=0),
                )
            sections = []

    def window_of(act, a):
        return jnp.concatenate(
            [act[dy, pl.ds((a + da) * dense, dense), :] for da in range(3) for dy in range(3)],
            axis=0,
        )

    def conv(matrix, acts, bias, a):
        cols = []
        for b in range(a, a + WIDE):
            parts = [window_of(x, b) for x in acts]
            cols.append(jnp.concatenate(parts, axis=0) if len(parts) > 1 else parts[0])
        got = jnp.dot(matrix[...], jnp.concatenate(cols, axis=1), preferred_element_type=F32)
        wide = jnp.concatenate([bias] * WIDE, axis=1)
        return jnp.maximum(got + wide, 0.0)

    def layer(matrix, acts, bias, result, tasks):
        for a in range(0, along, WIDE):
            got = conv(matrix, acts, bias, a)
            run(tasks, a // WIDE, along // WIDE)
            for h in range(WIDE):
                put_shifted(result, (1 + a + h) * dense, got[:, h * LANES : (h + 1) * LANES])

    def deep_rows(a):
        value = jnp.concatenate([gathered(z, a)[:chans] for z in range(depth)], axis=0)
        put_shifted(xd, (a + 1) * dense, value)

    tasks = matrix_tasks(p3, q3, m3) + [functools.partial(spread_cells, deep_v)] + [functools.partial(deep_rows, a) for a in range(along)]
    layer(m2, [x1], bias2, x2, tasks)
    pad_taps(w4_v, p4)
    tasks = matrix_tasks(p4, q4, m4)
    layer(m3, [x2, xd], bias3, x3, tasks)
    bias = bias4
    kinds = hw.shape[0]
    tap = hw[...].astype(F32)
    for z in range(depth):
        head[z * 4 : z * 4 + kinds, z * chans : (z + 1) * chans] = tap
    head_b = head[:, 0:dense].astype(BF)
    head_bias = column(hb, pad, 4 * depth, lambda r: r % 4)
    sz, sa = bump(depth), bump(along)
    row = lax.broadcasted_iota(jnp.int32, (4 * depth, LANES), 0)
    blend_z = jnp.full((4 * depth, LANES), float(sz[0]), F32)
    for z in range(1, depth):
        blend_z = jnp.where(row >= 4 * z, float(sz[z]), blend_z)
    across = jnp.broadcast_to(wy[...], (4 * depth, LANES))
    start = first_block[patch]
    move = offset[patch]
    base = lax.rem(start, owners)
    firsts = column(firsts_v, pad, firsts_v.shape[1], own)
    tasks = [functools.partial(make_adder, b, firsts) for b in range(adder.shape[1] // LANES)]
    for a in range(0, along, WIDE):
        fourth = conv(m4, [x3, x1], bias, a).astype(BF)
        logits = jnp.dot(head_b, fourth, preferred_element_type=F32) + head_bias
        run(tasks, a // WIDE, along // WIDE)
        value = jax.nn.sigmoid(logits)
        for h in range(WIDE):
            part = value[:, h * LANES : (h + 1) * LANES] * (
                blend_z * float(sa[a + h]) * across
            )
            place = move + (a + h)
            owner = base + lax.div(place, CW)
            owner = jnp.where(owner >= owners, owner - owners, owner)
            spot = owner * ROWS + lax.rem(place, CW)
            for z in range(depth):
                for kind in range(kinds):
                    r = z * 4 + kind
                    canvas[pl.ds(spot + (z * owners * ROWS + kind * CW), 1), :] = part[r : r + 1, :]
    for slot in range(out.shape[0]):
        out[slot] = canvas[slot * ROWS : (slot + 1) * ROWS, :].astype(BF)


def blend_kernel(adder, mine, out):
    rows = mine[...].reshape(mine.shape[0] * ROWS, LANES)
    total = jnp.dot(adder[...], rows, preferred_element_type=F32)
    for i in range(out.shape[0]):
        for kind in range(out.shape[1]):
            lo = i * ROWS + kind * CW
            out[i, kind] = total[lo : lo + CW, :]


def held_in(space, *arrays):
    return [pltpu.with_memory_space_constraint(a, space) for a in arrays]


def per_device(
    features,
    deep_path,
    weight_first,
    bias_first,
    weight_second,
    bias_second,
    weight_third,
    bias_third,
    weight_fourth,
    bias_fourth,
    head_weight,
    head_bias,
    block_first,
    block_offset,
):
    segments = lax.axis_size("segment")
    owners = lax.axis_size("patch")
    count, chans, depth, along, across = features.shape
    kinds = head_weight.shape[0]
    assert count == segments and depth == segments and across == LANES
    assert block_first.shape[0] <= LANES and owners >= KMAX
    assert along % GROUP == 0 and kinds * CW <= ROWS and chans <= SLOT and depth * SLOT == LANES
    dense = depth * chans
    assert dense % TILE == 0

    def by_cell(values):
        rows = (count, chans, along * depth, across)
        return values.transpose(0, 1, 3, 2, 4).reshape(rows)

    vmem = pl.BlockSpec(memory_space=pltpu.VMEM)
    hbm = pl.BlockSpec(memory_space=pltpu.HBM)
    act = pltpu.VMEM((3, (along + 2) * dense, LANES), BF)
    one = pltpu.VMEM((dense, 9 * dense), BF)
    two = pltpu.VMEM((dense, 18 * dense), BF)
    wy = jnp.asarray(bump(across)).reshape(1, across)
    slots, adder = pl.pallas_call(
        functools.partial(unet_kernel, owners, depth),
        out_shape=(
            jax.ShapeDtypeStruct((segments * owners, ROWS, across), BF),
            jax.ShapeDtypeStruct((CH_DEV * ROWS, segments * owners * ROWS), BF),
        ),
        in_specs=[hbm] * 16,
        out_specs=(vmem, vmem),
        scratch_shapes=[
            pltpu.SMEM(block_first.shape, jnp.int32),
            pltpu.SMEM(block_first.shape, jnp.int32),
            pltpu.VMEM((1, block_first.shape[0]), jnp.int32),
            pltpu.VMEM((chans, along * depth, across), BF),
            pltpu.VMEM((chans, along * depth, across), BF),
            pltpu.VMEM(weight_first.shape, BF),
            pltpu.VMEM(weight_second.shape, BF),
            pltpu.VMEM(weight_third.shape, BF),
            pltpu.VMEM(weight_fourth.shape, BF),
            pltpu.VMEM((1, chans), F32),
            pltpu.VMEM((1, chans), F32),
            pltpu.VMEM((1, chans), F32),
            pltpu.VMEM((1, chans), F32),
            pltpu.VMEM(head_weight.shape, BF),
            pltpu.VMEM((1, kinds), F32),
            pltpu.VMEM((1, across), F32),
            pltpu.VMEM((SLOT * (along * depth + 1), LANES), F32),
            pltpu.VMEM((3, depth * (along + 2) * SLOT, LANES), BF),
            act,
            act,
            act,
            act,
            pltpu.VMEM((GROUP * SLOT, 5 * LANES), BF),
            one,
            two,
            two,
            pltpu.VMEM((9 * SLOT, LANES), BF),
            pltpu.VMEM((18 * SLOT, LANES), BF),
            pltpu.VMEM((18 * SLOT, LANES), BF),
            pltpu.VMEM((9, SLOT, LANES), BF),
            pltpu.VMEM((27, SLOT, LANES), BF),
            pltpu.VMEM((27, SLOT, LANES), BF),
            pltpu.VMEM((27, SLOT, LANES), BF),
            pltpu.VMEM((8, LANES), F32),
            pltpu.VMEM((4 * depth, LANES), F32),
            pltpu.VMEM((segments * owners * ROWS, LANES), F32),
            pltpu.SemaphoreType.DMA((16,)),
        ],
        compiler_params=pltpu.CompilerParams(vmem_limit_bytes=48 * 2**20),
    )(
        *held_in(
            pltpu.HBM,
        block_first,
        block_offset,
        block_first.reshape(1, -1),
        by_cell(features),
        by_cell(deep_path),
        weight_first,
        weight_second,
        weight_third,
        weight_fourth,
        bias_first.reshape(1, chans),
        bias_second.reshape(1, chans),
        bias_third.reshape(1, chans),
        bias_fourth.reshape(1, chans),
        head_weight,
        head_bias.reshape(1, kinds),
        wy,
        )
    )
    mine = lax.all_to_all(slots, ("segment", "patch"), split_axis=0, concat_axis=0, tiled=True)
    blended = pl.pallas_call(
        blend_kernel,
        out_shape=jax.ShapeDtypeStruct((CH_DEV, kinds, CW, across), F32),
        in_specs=[vmem, vmem],
        out_specs=vmem,
    )(*held_in(pltpu.VMEM, adder, mine))
    return blended.reshape(CH_DEV, 1, kinds, 1, CW, across)


def solution(mesh):
    rows = P("patch", None, None, None, None)
    return jax.shard_map(
        per_device,
        mesh=mesh,
        in_specs=(rows, rows) + (P(),) * 12,
        out_specs=P(None, "patch", None, "segment", None, None),
        check_vma=False,
    )
```

```python
import functools
import math

import jax
import jax.numpy as jnp
import numpy as np
from jax import lax
from jax.experimental import pallas as pl
from jax.experimental.pallas import tpu as pltpu
from jax.sharding import PartitionSpec as P

CW = 4
CH_DEV = 8
KMAX = 4
LANES = 128
SLOT = 32
TILE = 16
ROWS = 16
WIDE = 4
GROUP = 4
BF = jnp.bfloat16
F32 = jnp.float32


def bump(count):
    place = (np.arange(count).astype(np.float32) + np.float32(0.5)) / np.float32(count)
    return (np.sin(np.float32(np.pi) * place) ** 2).astype(np.float32)


def lane_index(rows):
    return lax.broadcasted_iota(jnp.int32, (rows, LANES), 1)


def lane_mask(low, high):
    lane = lane_index(TILE)
    return jnp.where((lane >= low) & (lane < high), 1.0, 0.0).astype(BF)


def masked(value, tile):
    rows = value.shape[0]
    return (value.reshape(rows // TILE, TILE, LANES) * tile[None]).reshape(rows, LANES)


def put_shifted(act, row, value):
    rows = value.shape[0]
    value = value.astype(BF)
    act[1, pl.ds(row, rows), :] = value
    act[0, pl.ds(row, rows), :] = masked(pltpu.roll(value, 1, 1), lane_mask(1, LANES))
    act[2, pl.ds(row, rows), :] = masked(
        pltpu.roll(value, LANES - 1, 1), lane_mask(0, LANES - 1)
    )


def turned(value, lanes):
    return pltpu.roll(value, lanes % LANES, 1) if lanes % LANES else value


def pad_taps(weight, padded):
    taps, rows, cols = weight.shape
    for t in range(taps):
        padded[t, 0:rows, 0:cols] = weight[t]


def build_bases(padded, low, chans, wide, bases, place, da):
    parts = []
    for dz in range(3):
        taps = padded[9 * dz + 3 * da : 9 * dz + 3 * da + 3].reshape(3 * SLOT, LANES)
        if low or wide:
            taps = masked(taps, lane_mask(low, low + chans))
        parts.append(turned(taps, dz * chans - low))
    first = (place + 3 * da) * SLOT
    bases[first : first + 3 * SLOT, :] = parts[0] + parts[1] + parts[2]


def build_rows(bases, blocks, chans, big, depth, z):
    dense = depth * chans
    columns = {}
    for k in range(blocks):
        moved = turned(bases[k * SLOT : (k + 1) * SLOT, :], k * dense + (z - 1) * chans)
        low = k * dense + max(z - 1, 0) * chans
        high = k * dense + min(z + 2, depth) * chans
        for j in range(low // LANES, (high - 1) // LANES + 1):
            tile = lane_mask(max(low - j * LANES, 0), min(high - j * LANES, LANES))
            piece = masked(moved, tile)
            columns[j] = columns[j] + piece if j in columns else piece
    for j, value in columns.items():
        lanes = min(LANES, blocks * dense - j * LANES)
        big[z * chans : (z + 1) * chans, j * LANES : j * LANES + lanes] = value[:chans, :lanes]


def build_first(padded, big):
    parts = [padded[3 * da : 3 * da + 3].reshape(3 * SLOT, LANES) for da in range(3)]
    base = parts[0] + turned(parts[1], SLOT) + turned(parts[2], 2 * SLOT)
    for a in range(GROUP):
        moved = turned(base, a * SLOT)
        wide = masked(moved, lane_mask(a * SLOT, LANES))
        rest = masked(moved, lane_mask(0, (a - 1) * SLOT))
        rows = slice(a * SLOT, (a + 1) * SLOT)
        for dy in range(3):
            big[rows, dy * LANES : (dy + 1) * LANES] = wide[dy * SLOT : (dy + 1) * SLOT]
        half = [rest[dy * SLOT : (dy + 1) * SLOT] for dy in range(3)]
        big[rows, 3 * LANES : 4 * LANES] = half[0] + turned(half[1], LANES // 2)
        big[rows, 4 * LANES : 5 * LANES] = half[2]


def column(row_ref, pad, rows, pick):
    pad[...] = jnp.zeros(pad.shape, F32)
    pad[0:1, 0 : row_ref.shape[1]] = row_ref[...].astype(F32)
    spread = jnp.broadcast_to(pad[0:1, :], (rows, LANES))
    want = pick(lax.broadcasted_iota(jnp.int32, (rows, LANES), 0))
    return jnp.sum(jnp.where(lane_index(rows) == want, spread, 0.0), axis=1, keepdims=True)


def unet_kernel(
    owners,
    depth,
    first_block_h,
    offset_h,
    firsts_h,
    features,
    deep,
    w1,
    w2,
    w3,
    w4,
    b1_h,
    b2_h,
    b3_h,
    b4_h,
    hw_h,
    hb_h,
    wy_h,
    out,
    adder,
    first_block,
    offset,
    firsts_v,
    feat_v,
    deep_v,
    w1_v,
    w2_v,
    w3_v,
    w4_v,
    b1,
    b2,
    b3,
    b4,
    hw,
    hb,
    wy,
    cells,
    xf,
    x1,
    x2,
    xd,
    x3,
    m1,
    m2,
    m3,
    m4,
    q2,
    q3,
    q4,
    p1,
    p2,
    p3,
    p4,
    pad,
    head,
    canvas,
    sems,
):
    chans, along, depth = feat_v.shape[0], feat_v.shape[1] // depth, depth
    dense = depth * chans
    me = lax.axis_index("segment")
    patch = lax.axis_index("patch") * features.shape[0] + me

    copies = [
        pltpu.make_async_copy(src, dst, sems.at[i])
        for i, (src, dst) in enumerate(
            [
                (w1, w1_v),
                (features.at[me], feat_v),
                (w2, w2_v),
                (b1_h, b1),
                (w3, w3_v),
                (deep.at[me], deep_v),
                (w4, w4_v),
                (b2_h, b2),
                (b3_h, b3),
                (b4_h, b4),
                (hw_h, hw),
                (hb_h, hb),
                (wy_h, wy),
                (first_block_h, first_block),
                (offset_h, offset),
                (firsts_h, firsts_v),
            ]
        )
    ]
    for c in copies:
        c.start()

    for act in (x1, x2, xd, x3):
        for dy in range(3):
            act[dy, 0:dense, :] = jnp.zeros((dense, LANES), BF)
            act[dy, (along + 1) * dense : (along + 2) * dense, :] = jnp.zeros((dense, LANES), BF)
    high = (along + 2) * SLOT
    for dy in range(3):
        for z in range(depth):
            xf[dy, z * high : z * high + SLOT, :] = jnp.zeros((SLOT, LANES), BF)
            xf[dy, (z + 1) * high - SLOT : (z + 1) * high, :] = jnp.zeros((SLOT, LANES), BF)
    for padded in (p1, p2, p3, p4):
        padded[...] = jnp.zeros(padded.shape, BF)
    head[...] = jnp.zeros(head.shape, F32)
    canvas[...] = jnp.zeros(canvas.shape, F32)
    pitch = cells.shape[0] // SLOT
    used = chans * pitch
    cells[used:, :] = jnp.zeros((cells.shape[0] - used, LANES), F32)

    def spread_cells(source):
        for c in range(chans):
            cells[pl.ds(c * pitch, along * depth), :] = source[c].astype(F32)

    def gathered(z, a):
        return cells[pl.ds(a * depth + z, SLOT, stride=pitch), :]

    def own(r):
        return r

    def make_adder(block, firsts):
        patches = firsts.shape[0]
        each = LANES // ROWS
        src = block * each + lane_index(patches) // ROWS
        sender = (src % owners) * features.shape[0] + src // owners
        mine = lax.broadcasted_iota(jnp.int32, (patches, LANES), 0) == sender
        first = jnp.sum(jnp.where(mine, firsts, 0.0), axis=0, keepdims=True).astype(jnp.int32)
        row = lax.broadcasted_iota(jnp.int32, (adder.shape[0], LANES), 0)
        lane = lane_index(adder.shape[0])
        ahead = (row // ROWS) * owners + lax.axis_index("patch") - first
        keep = (ahead >= 0) & (ahead < KMAX) & (row % ROWS == lane % ROWS)
        adder[:, block * LANES : (block + 1) * LANES] = jnp.where(keep, 1.0, 0.0).astype(BF)

    def matrix_tasks(padded, bases, big):
        sources = big.shape[1] // (9 * dense)
        tasks = [
            functools.partial(
                build_bases, padded, i * chans, chans, sources > 1, bases, 9 * i, da
            )
            for i in range(sources)
            for da in range(3)
        ]
        return tasks + [
            functools.partial(build_rows, bases, 9 * sources, chans, big, depth, z)
            for z in range(depth)
        ]

    for c in copies[0:2]:
        c.wait()
    pad_taps(w1_v, p1)
    build_first(p1, m1)
    spread_cells(feat_v)
    for z in range(depth):
        for a in range(along):
            put_shifted(xf, z * high + (a + 1) * SLOT, gathered(z, a))

    for c in copies[2:]:
        c.wait()
    def bias_rows(ref, rows, each):
        return jnp.broadcast_to(column(ref, pad, rows, lambda r: r % each), (rows, LANES))

    def run(tasks, step, steps):
        for task in tasks[len(tasks) * step // steps : len(tasks) * (step + 1) // steps]:
            task()

    bias = bias_rows(b1, GROUP * SLOT, SLOT)
    bias2, bias3, bias4 = (bias_rows(b, dense, chans) for b in (b2, b3, b4))
    tasks = [functools.partial(pad_taps, w2_v, p2)] + matrix_tasks(p2, q2, m2) + [functools.partial(pad_taps, w3_v, p3)]
    columns = [(z, group) for group in range(along // GROUP) for z in range(depth)]

    def first_window(z, group):
        low = z * high + group * GROUP * SLOT
        pieces = [xf[dy, pl.ds(low, LANES), :] for dy in range(3)]
        pieces += [xf[dy, pl.ds(low + LANES, LANES // 2), :] for dy in range(3)]
        return jnp.concatenate(pieces, axis=0)

    sections = []
    for pair in range(0, len(columns), depth):
        rhs = jnp.concatenate([first_window(*c) for c in columns[pair : pair + depth]], axis=1)
        got = jnp.dot(m1[:, 0 : rhs.shape[0]], rhs, preferred_element_type=F32)
        run(tasks, pair // depth, len(columns) // depth)
        for h, (z, group) in enumerate(columns[pair : pair + depth]):
            sections.append(jnp.maximum(got[:, h * LANES : (h + 1) * LANES] + bias, 0.0))
            if len(sections) < depth:
                continue
            for a in range(GROUP):
                low = a * SLOT
                put_shifted(
                    x1,
                    (1 + group * GROUP + a) * dense,
                    jnp.concatenate([part[low : low + chans] for part in sections], axis=0),
                )
            sections = []

    def window_of(act, a):
        return jnp.concatenate(
            [act[dy, pl.ds((a + da) * dense, dense), :] for da in range(3) for dy in range(3)],
            axis=0,
        )

    def conv(matrix, acts, bias, a):
        cols = []
        for b in range(a, a + WIDE):
            parts = [window_of(x, b) for x in acts]
            cols.append(jnp.concatenate(parts, axis=0) if len(parts) > 1 else parts[0])
        got = jnp.dot(matrix[...], jnp.concatenate(cols, axis=1), preferred_element_type=F32)
        wide = jnp.concatenate([bias] * WIDE, axis=1)
        return jnp.maximum(got + wide, 0.0)

    def layer(matrix, acts, bias, result, tasks):
        for a in range(0, along, WIDE):
            got = conv(matrix, acts, bias, a)
            run(tasks, a // WIDE, along // WIDE)
            for h in range(WIDE):
                put_shifted(result, (1 + a + h) * dense, got[:, h * LANES : (h + 1) * LANES])

    def deep_rows(a):
        value = jnp.concatenate([gathered(z, a)[:chans] for z in range(depth)], axis=0)
        put_shifted(xd, (a + 1) * dense, value)

    tasks = matrix_tasks(p3, q3, m3) + [functools.partial(spread_cells, deep_v)] + [functools.partial(deep_rows, a) for a in range(along)]
    layer(m2, [x1], bias2, x2, tasks)
    pad_taps(w4_v, p4)
    tasks = matrix_tasks(p4, q4, m4)
    layer(m3, [x2, xd], bias3, x3, tasks)
    bias = bias4
    kinds = hw.shape[0]
    tap = hw[...].astype(F32)
    for z in range(depth):
        head[z * 4 : z * 4 + kinds, z * chans : (z + 1) * chans] = tap
    head_b = head[:, 0:dense].astype(BF)
    head_bias = column(hb, pad, 4 * depth, lambda r: r % 4)
    sz, sa = bump(depth), bump(along)
    row = lax.broadcasted_iota(jnp.int32, (4 * depth, LANES), 0)
    blend_z = jnp.full((4 * depth, LANES), float(sz[0]), F32)
    for z in range(1, depth):
        blend_z = jnp.where(row >= 4 * z, float(sz[z]), blend_z)
    across = jnp.broadcast_to(wy[...], (4 * depth, LANES))
    start = first_block[patch]
    move = offset[patch]
    base = lax.rem(start, owners)
    firsts = column(firsts_v, pad, firsts_v.shape[1], own)
    tasks = [functools.partial(make_adder, b, firsts) for b in range(adder.shape[1] // LANES)]
    for a in range(0, along, WIDE):
        fourth = conv(m4, [x3, x1], bias, a).astype(BF)
        logits = jnp.dot(head_b, fourth, preferred_element_type=F32) + head_bias
        run(tasks, a // WIDE, along // WIDE)
        value = jax.nn.sigmoid(logits)
        for h in range(WIDE):
            part = value[:, h * LANES : (h + 1) * LANES] * (
                blend_z * float(sa[a + h]) * across
            )
            place = move + (a + h)
            owner = base + lax.div(place, CW)
            owner = jnp.where(owner >= owners, owner - owners, owner)
            spot = owner * ROWS + lax.rem(place, CW)
            for z in range(depth):
                for kind in range(kinds):
                    r = z * 4 + kind
                    canvas[pl.ds(spot + (z * owners * ROWS + kind * CW), 1), :] = part[r : r + 1, :]
    for slot in range(out.shape[0]):
        out[slot] = canvas[slot * ROWS : (slot + 1) * ROWS, :].astype(BF)


def blend_kernel(adder, mine, out):
    rows = mine[...].reshape(mine.shape[0] * ROWS, LANES)
    total = jnp.dot(adder[...], rows, preferred_element_type=F32)
    for i in range(out.shape[0]):
        for kind in range(out.shape[1]):
            lo = i * ROWS + kind * CW
            out[i, kind] = total[lo : lo + CW, :]


def held_in(space, *arrays):
    return [pltpu.with_memory_space_constraint(a, space) for a in arrays]


def per_device(
    features,
    deep_path,
    weight_first,
    bias_first,
    weight_second,
    bias_second,
    weight_third,
    bias_third,
    weight_fourth,
    bias_fourth,
    head_weight,
    head_bias,
    block_first,
    block_offset,
):
    segments = lax.axis_size("segment")
    owners = lax.axis_size("patch")
    count, chans, depth, along, across = features.shape
    kinds = head_weight.shape[0]
    assert count == segments and depth == segments and across == LANES
    assert block_first.shape[0] <= LANES and owners >= KMAX
    assert along % GROUP == 0 and kinds * CW <= ROWS and chans <= SLOT and depth * SLOT == LANES
    dense = depth * chans
    assert dense % TILE == 0

    def by_cell(values):
        rows = (count, chans, along * depth, across)
        return values.transpose(0, 1, 3, 2, 4).reshape(rows)

    vmem = pl.BlockSpec(memory_space=pltpu.VMEM)
    hbm = pl.BlockSpec(memory_space=pltpu.HBM)
    act = pltpu.VMEM((3, (along + 2) * dense, LANES), BF)
    one = pltpu.VMEM((dense, 9 * dense), BF)
    two = pltpu.VMEM((dense, 18 * dense), BF)
    wy = jnp.asarray(bump(across)).reshape(1, across)
    slots, adder = pl.pallas_call(
        functools.partial(unet_kernel, owners, depth),
        out_shape=(
            jax.ShapeDtypeStruct((segments * owners, ROWS, across), BF),
            jax.ShapeDtypeStruct((CH_DEV * ROWS, segments * owners * ROWS), BF),
        ),
        in_specs=[hbm] * 16,
        out_specs=(vmem, vmem),
        scratch_shapes=[
            pltpu.SMEM(block_first.shape, jnp.int32),
            pltpu.SMEM(block_first.shape, jnp.int32),
            pltpu.VMEM((1, block_first.shape[0]), jnp.int32),
            pltpu.VMEM((chans, along * depth, across), BF),
            pltpu.VMEM((chans, along * depth, across), BF),
            pltpu.VMEM(weight_first.shape, BF),
            pltpu.VMEM(weight_second.shape, BF),
            pltpu.VMEM(weight_third.shape, BF),
            pltpu.VMEM(weight_fourth.shape, BF),
            pltpu.VMEM((1, chans), F32),
            pltpu.VMEM((1, chans), F32),
            pltpu.VMEM((1, chans), F32),
            pltpu.VMEM((1, chans), F32),
            pltpu.VMEM(head_weight.shape, BF),
            pltpu.VMEM((1, kinds), F32),
            pltpu.VMEM((1, across), F32),
            pltpu.VMEM((SLOT * (along * depth + 1), LANES), F32),
            pltpu.VMEM((3, depth * (along + 2) * SLOT, LANES), BF),
            act,
            act,
            act,
            act,
            pltpu.VMEM((GROUP * SLOT, 5 * LANES), BF),
            one,
            two,
            two,
            pltpu.VMEM((9 * SLOT, LANES), BF),
            pltpu.VMEM((18 * SLOT, LANES), BF),
            pltpu.VMEM((18 * SLOT, LANES), BF),
            pltpu.VMEM((9, SLOT, LANES), BF),
            pltpu.VMEM((27, SLOT, LANES), BF),
            pltpu.VMEM((27, SLOT, LANES), BF),
            pltpu.VMEM((27, SLOT, LANES), BF),
            pltpu.VMEM((8, LANES), F32),
            pltpu.VMEM((4 * depth, LANES), F32),
            pltpu.VMEM((segments * owners * ROWS, LANES), F32),
            pltpu.SemaphoreType.DMA((16,)),
        ],
        compiler_params=pltpu.CompilerParams(vmem_limit_bytes=48 * 2**20),
    )(
        *held_in(
            pltpu.HBM,
        block_first,
        block_offset,
        block_first.reshape(1, -1),
        by_cell(features),
        by_cell(deep_path),
        weight_first,
        weight_second,
        weight_third,
        weight_fourth,
        bias_first.reshape(1, chans),
        bias_second.reshape(1, chans),
        bias_third.reshape(1, chans),
        bias_fourth.reshape(1, chans),
        head_weight,
        head_bias.reshape(1, kinds),
        wy,
        )
    )
    mine = lax.all_to_all(slots, ("segment", "patch"), split_axis=0, concat_axis=0, tiled=True)
    blended = pl.pallas_call(
        blend_kernel,
        out_shape=jax.ShapeDtypeStruct((CH_DEV, kinds, CW, across), F32),
        in_specs=[vmem, vmem],
        out_specs=vmem,
    )(*held_in(pltpu.VMEM, adder, mine))
    return blended.reshape(CH_DEV, 1, kinds, 1, CW, across)


def solution(mesh):
    rows = P("patch", None, None, None, None)
    return jax.shard_map(
        per_device,
        mesh=mesh,
        in_specs=(rows, rows) + (P(),) * 12,
        out_specs=P(None, "patch", None, "segment", None, None),
        check_vma=False,
    )
```
